32 devices in a mesh: grp: 2 (over y), row: 8 (over z, x), sub: 2 (over core).
Axes of the slice: x: 2, y: 2, z: 4, core: 2. Of those that a mesh axis runs over, the one named last changes fastest.
Arguments:
- pair_rep: bfloat16 [64, 32, 128], P(('grp', 'row'), 'sub'), parts along dimension 0, may hold values from -6 to 6
- norm_gain: float32 [128], replicated, may hold values from 0.1 to 1.9
- norm_bias: float32 [128], replicated, may hold values from -3 to 3
- w_a_proj: bfloat16 [128, 128], replicated, may hold values from -0.5 to 0.5
- w_a_gate: bfloat16 [128, 128], replicated, may hold values from -0.5 to 0.5
- w_b_proj: bfloat16 [128, 128], replicated, may hold values from -0.5 to 0.5
- w_b_gate: bfloat16 [128, 128], replicated, may hold values from -0.5 to 0.5
- w_gate: bfloat16 [128, 128], replicated, may hold values from -0.5 to 0.5
- out_gain: float32 [128], replicated, may hold values from 0.1 to 1.9
- out_bias: float32 [128], replicated, may hold values from -3 to 3
- w_out: bfloat16 [128, 128], replicated, may hold values from -0.5 to 0.5
Outputs:
- update: bfloat16 [64, 32, 128], P(('grp', 'row'), 'sub'), parts along dimension 0
The draws below stay inside these ranges and needn't reach their ends.
There are 2 independent parts, one for each index of `grp`. The reference program is written for one: setup_inputs(seed, part) draws one part's arguments, and reference() takes and returns one part's arrays. A program takes and returns all parts, laid end to end along the dimension named above; an argument that names none is the same for every part. Nothing has to cross between parts.
All inputs are finite; a program needn't handle non-finite values.
Results may differ from the reference program's by a relative error of at most 0.012.
Values may be sent and summed in bfloat16 or wider, within the bound.
A program may use at most 64 MiB of HBM per device.

```python
import jax
import jax.numpy as jnp
from jax import lax

C = 128
H = 128
ROWS_DEV = 4
TOKENS = 32
N_ROW = 8


def block_levels(stream_key, dims, pieces, least, high):
    def one(position, blocks):
        heights = jax.random.uniform(jax.random.fold_in(jax.random.fold_in(stream_key, 6), position), (blocks,), jnp.float32, least / len(pieces), high / len(pieces))
        return jnp.repeat(jnp.exp(heights), dims[position] // blocks).reshape((-1,) + (1,) * (len(dims) - position - 1))

    level = one(*pieces[0])
    for cut in pieces[1:]:
        level = level * one(*cut)
    return level


def bell_draw(rng, shape, deviation, most, split=(), dtype=jnp.bfloat16):
    level = block_levels(rng, shape, split, -0.22, 0.18) if split else 1.0
    entries = jax.random.normal(rng, shape, jnp.float32) * deviation * level
    return jnp.minimum(jnp.maximum(entries, -most), most).astype(dtype)


def setup_inputs(seed: int = 0, part: int = 0) -> dict:
    key_list = jax.random.split(jax.random.key(seed), 12)
    part_keys = jax.random.split(jax.random.fold_in(key_list[11], part), 12)
    pair_rep = bell_draw(part_keys[0], (TOKENS, TOKENS, C), 1.0, 6.0, ((0, 8), (1, 2)))
    norm_gain = jnp.clip(1.0 + 0.18 * jax.random.normal(key_list[1], (C,), jnp.float32), 0.1, 1.9)
    norm_bias = bell_draw(key_list[2], (C,), 0.5, 3.0, (), jnp.float32)
    w_a_proj = bell_draw(key_list[3], (C, H), C ** -0.5, 0.5)
    w_a_gate = bell_draw(key_list[4], (C, H), C ** -0.5, 0.5)
    w_b_proj = bell_draw(key_list[5], (C, H), C ** -0.5, 0.5)
    w_b_gate = bell_draw(key_list[6], (C, H), C ** -0.5, 0.5)
    w_gate = bell_draw(key_list[7], (C, C), C ** -0.5, 0.5)
    out_gain = jnp.clip(1.0 + 0.18 * jax.random.normal(key_list[8], (H,), jnp.float32), 0.1, 1.9)
    out_bias = bell_draw(key_list[9], (H,), 0.5, 3.0, (), jnp.float32)
    w_out = bell_draw(key_list[10], (H, C), H ** -0.5, 0.5)
    return dict(pair_rep=pair_rep, norm_gain=norm_gain, norm_bias=norm_bias, w_a_proj=w_a_proj, w_a_gate=w_a_gate, w_b_proj=w_b_proj, w_b_gate=w_b_gate, w_gate=w_gate, out_gain=out_gain, out_bias=out_bias, w_out=w_out)


EPSILON = 1e-05

def layer_norm(values, gain, shift, axis):
    centred = values - lax.optimization_barrier(jnp.mean(values, axis=axis, keepdims=True))
    variance = lax.optimization_barrier(jnp.mean(centred * centred, axis=axis, keepdims=True))
    return centred * lax.rsqrt(variance + EPSILON) * gain + shift

def reference(pair_rep, norm_gain, norm_bias, w_a_proj, w_a_gate, w_b_proj, w_b_gate, w_gate, out_gain, out_bias, w_out):
    w_inner = jnp.concatenate([w_a_proj, w_a_gate, w_b_proj, w_b_gate], axis=1)

    def project(block):
        normed = layer_norm(block.astype(jnp.float32), norm_gain, norm_bias, -1).astype(jnp.bfloat16)
        flat_rows = normed.reshape(-1, C)
        inner = jnp.dot(flat_rows, w_inner, preferred_element_type=jnp.float32)
        left_act = (jax.nn.sigmoid(inner[:, H:2 * H]) * inner[:, :H]).astype(jnp.bfloat16)
        right_act = (jax.nn.sigmoid(inner[:, 3 * H:4 * H]) * inner[:, 2 * H:3 * H]).astype(jnp.bfloat16)
        gating = jax.nn.sigmoid(jnp.dot(flat_rows, w_gate, preferred_element_type=jnp.float32)).astype(jnp.bfloat16)
        return (left_act.reshape(ROWS_DEV, TOKENS, H), right_act.reshape(ROWS_DEV, TOKENS, H), gating.reshape(ROWS_DEV, TOKENS, C))
    blocks = pair_rep.reshape(N_ROW, ROWS_DEV, TOKENS, C)
    left_act, right_act, gating = lax.map(project, blocks)
    left_t = jnp.transpose(left_act.reshape(TOKENS, TOKENS, H), (2, 0, 1))
    right_t = jnp.transpose(right_act.reshape(TOKENS, TOKENS, H), (2, 0, 1))

    def channel(operands):
        left_one, right_one = operands
        return jnp.dot(left_one, right_one.T, preferred_element_type=jnp.float32).astype(jnp.bfloat16)
    triangle = lax.map(channel, (left_t, right_t))
    tri_rows = jnp.transpose(triangle, (1, 2, 0)).reshape(N_ROW, ROWS_DEV, TOKENS, H)

    def finish(operands):
        tri_block, gate_block = operands
        normed = layer_norm(tri_block.astype(jnp.float32), out_gain, out_bias, -1).astype(jnp.bfloat16)
        mixed = jnp.dot(normed.reshape(-1, H), w_out, preferred_element_type=jnp.float32)
        result = gate_block.reshape(-1, C).astype(jnp.float32) * mixed
        return result.astype(jnp.bfloat16).reshape(ROWS_DEV, TOKENS, C)
    return lax.map(finish, (tri_rows, gating)).reshape(TOKENS, TOKENS, C)
```

```python
import functools

import jax
import jax.numpy as jnp
from jax import lax
from jax.experimental import pallas as pl
from jax.experimental.pallas import tpu as pltpu
from jax.sharding import PartitionSpec as P

EPSILON = 1e-05


def layer_norm(values, gain, shift, axis):
    centred = values - jnp.mean(values, axis=axis, keepdims=True)
    variance = jnp.mean(centred * centred, axis=axis, keepdims=True)
    return centred * lax.rsqrt(variance + EPSILON) * gain + shift


def per_device(
    pair_rep,
    norm_gain,
    norm_bias,
    w_a_proj,
    w_a_gate,
    w_b_proj,
    w_b_gate,
    w_gate,
    out_gain,
    out_bias,
    w_out,
):
    hidden = w_a_proj.shape[1]
    w_inner = jnp.concatenate([w_a_proj, w_a_gate, w_b_proj, w_b_gate], axis=1)
    normed = layer_norm(pair_rep.astype(jnp.float32), norm_gain, norm_bias, -1).astype(jnp.bfloat16)
    inner = jnp.einsum("rkc,cm->mrk", normed, w_inner, preferred_element_type=jnp.float32)
    left_local = (jax.nn.sigmoid(inner[hidden : 2 * hidden]) * inner[:hidden]).astype(jnp.bfloat16)
    right_local = (
        jax.nn.sigmoid(inner[3 * hidden : 4 * hidden]) * inner[2 * hidden : 3 * hidden]
    ).astype(jnp.bfloat16)
    gating = jax.nn.sigmoid(
        jnp.einsum("rkc,cd->rkd", normed, w_gate, preferred_element_type=jnp.float32)
    ).astype(jnp.bfloat16)
    left_chan, right_chan = (
        lax.all_to_all(left_local, "row", split_axis=0, concat_axis=1, tiled=True),
        lax.all_to_all(right_local, "row", split_axis=0, concat_axis=1, tiled=True),
    )
    left_rows = lax.all_to_all(left_chan, "sub", split_axis=1, concat_axis=2, tiled=True)
    triangle = jnp.einsum(
        "hik,hjk->hij",
        left_rows,
        lax.all_gather(right_chan, "sub", axis=2, tiled=True),
        preferred_element_type=jnp.float32,
    ).astype(jnp.bfloat16)
    regrouped = lax.all_to_all(
        lax.all_to_all(triangle, "sub", split_axis=2, concat_axis=1, tiled=True),
        "row",
        split_axis=1,
        concat_axis=0,
        tiled=True,
    )
    hidden_normed = layer_norm(
        regrouped.astype(jnp.float32), out_gain[:, None, None], out_bias[:, None, None], 0
    ).astype(jnp.bfloat16)
    mixed = jnp.einsum("hrj,hc->rjc", hidden_normed, w_out, preferred_element_type=jnp.float32)
    return (gating.astype(jnp.float32) * mixed).astype(jnp.bfloat16)


def gated(normed, weights):
    hidden = weights.shape[1] // 2
    inner = jnp.dot(normed, weights, preferred_element_type=jnp.float32)
    return (jax.nn.sigmoid(inner[:, hidden:]) * inner[:, :hidden]).astype(jnp.bfloat16)


def kernel(
    n_row,
    pair_hbm,
    ngain_hbm,
    nbias_hbm,
    wap_hbm,
    wag_hbm,
    wbp_hbm,
    wbg_hbm,
    wg_hbm,
    ogain_hbm,
    obias_hbm,
    wo_hbm,
    out_ref,
    pair_v,
    vec_v,
    w_v,
    wo_v,
    right_send,
    right_buf,
    left_buf,
    tri_v,
    in_sem,
    send_sem,
    recv_sem,
    left_sem,
    ready,
    late,
):
    rows, cols, chan = pair_v.shape
    hidden = right_send.shape[-1]
    half = n_row // 2
    row = lax.axis_index("row")
    sub = lax.axis_index("sub")
    other = 1 - sub
    owner = row // half
    slot = lax.rem(row, half)
    near = sub == owner
    low = owner == 0
    low_near = jnp.logical_and(low, sub == 0)
    low_far = jnp.logical_and(low, sub == 1)
    high_near = jnp.logical_and(owner == 1, sub == 1)
    high_far = jnp.logical_and(owner == 1, sub == 0)
    last = row == n_row - 1
    split = half // 2
    mid = jnp.logical_and(owner == 1, slot < split)
    outer = jnp.logical_and(owner == 1, jnp.logical_and(slot >= split, jnp.logical_not(last)))

    loads = [
        pltpu.make_async_copy(pair_hbm, pair_v, in_sem.at[0]),
        pltpu.make_async_copy(ngain_hbm, vec_v.at[0], in_sem.at[1]),
        pltpu.make_async_copy(nbias_hbm, vec_v.at[1], in_sem.at[2]),
        pltpu.make_async_copy(wbp_hbm, w_v.at[:, 0:hidden], in_sem.at[3]),
        pltpu.make_async_copy(wbg_hbm, w_v.at[:, hidden : 2 * hidden], in_sem.at[4]),
        pltpu.make_async_copy(wap_hbm, w_v.at[:, 2 * hidden : 3 * hidden], in_sem.at[5]),
        pltpu.make_async_copy(wag_hbm, w_v.at[:, 3 * hidden : 4 * hidden], in_sem.at[6]),
        pltpu.make_async_copy(wg_hbm, w_v.at[:, 4 * hidden : 4 * hidden + chan], in_sem.at[7]),
        pltpu.make_async_copy(ogain_hbm, vec_v.at[2], in_sem.at[8]),
        pltpu.make_async_copy(obias_hbm, vec_v.at[3], in_sem.at[9]),
        pltpu.make_async_copy(wo_hbm, wo_v, in_sem.at[10]),
    ]
    for load in loads:
        load.start()

    barrier = pltpu.get_barrier_semaphore()

    def greet(semaphore, target):
        pl.semaphore_signal(
            semaphore, inc=1, device_id=target, device_id_type=pl.DeviceIdType.MESH
        )

    @pl.when(low_near)
    def _():
        for step in range(1, half):
            greet(barrier, {"row": lax.rem(slot + step, half), "sub": 0})

    @pl.when(low_far)
    def _():
        greet(barrier, {"sub": 0})
        for step in range(half)[::-1]:
            greet(barrier, {"row": half + step, "sub": 0})
            if step >= split:
                greet(barrier, {"row": half + step, "sub": 1})

    @pl.when(jnp.logical_and(high_far, jnp.logical_not(last)))
    def _():
        for step in range(half):
            greet(barrier, {"row": step, "sub": 1})

    @pl.when(high_near)
    def _():
        greet(barrier, {"sub": 0})
        for step in range(half):

            @pl.when(slot != step)
            def _():
                greet(barrier, {"row": half + step, "sub": 1})
                if step >= split:
                    greet(barrier, {"row": half + step, "sub": 0})

    left_copy = pltpu.make_async_remote_copy(
        src_ref=left_buf.at[sub],
        dst_ref=left_buf.at[sub],
        send_sem=send_sem.at[n_row],
        recv_sem=left_sem,
        device_id={"sub": other},
        device_id_type=pl.DeviceIdType.MESH,
    )

    def block_copy(source, index, target_row, target_sub):
        return pltpu.make_async_remote_copy(
            src_ref=source,
            dst_ref=right_buf.at[slot, sub],
            send_sem=send_sem.at[index],
            recv_sem=recv_sem.at[slot, sub],
            device_id={"row": target_row, "sub": target_sub},
            device_id_type=pl.DeviceIdType.MESH,
        )

    raw_copy = block_copy(pair_hbm, 0, 0, owner)
    copies = [block_copy(right_send, q, q, owner) for q in range(n_row)]
    copies[half:] = [
        block_copy(right_send, q, q, jnp.where(low, 0, 1)) for q in range(half, n_row)
    ]
    sent = [jnp.logical_not(jnp.logical_and(near, row == q)) for q in range(n_row)]

    def start(first, end, guarded):
        for q in range(first, end):
            if guarded:

                @pl.when(sent[q])
                def _():
                    copies[q].start()
            else:
                copies[q].start()

    @pl.when(low_near)
    def _():
        pl.semaphore_wait(barrier, half)
        greet(ready, {"sub": 1})

    @pl.when(jnp.logical_and(high_far, mid))
    def _():
        pl.semaphore_wait(barrier, half + 1)
        greet(ready, {"sub": 1})

    @pl.when(last)
    def _():
        pl.semaphore_wait(barrier, 2 * half - sub)
        raw_copy.start()

        @pl.when(sub == 0)
        def _():
            greet(ready, {"sub": 1})
            for step in range(half):
                greet(late, {"row": step, "sub": 1})

    for load in loads[:3]:
        load.wait()
    pair = pair_v[...].astype(jnp.float32).reshape(rows * cols, chan)
    normed = layer_norm(pair, vec_v[0], vec_v[1], -1).astype(jnp.bfloat16)
    for load in loads[3:5]:
        load.wait()
    right = gated(normed, w_v[:, 0 : 2 * hidden]).reshape(rows, cols, hidden)
    right_send[...] = right

    @pl.when(low_far)
    def _():
        pl.semaphore_wait(ready, 1)

    @pl.when(jnp.logical_and(high_near, mid))
    def _():
        pl.semaphore_wait(ready, 1)

    @pl.when(outer)
    def _():
        pl.semaphore_wait(barrier, 2 * half - sub)

        @pl.when(sub == 0)
        def _():
            greet(ready, {"sub": 1})

    @pl.when(jnp.logical_and(sent[0], jnp.logical_not(last)))
    def _():
        copies[0].start()

    start(1, half, True)

    @pl.when(near)
    def _():
        right_buf[slot, sub] = right

    for load in loads[5:7]:
        load.wait()
    left = gated(normed, w_v[:, 2 * hidden : 4 * hidden])
    left_buf[sub] = left.reshape(rows, cols, hidden)

    @pl.when(jnp.logical_and(high_near, jnp.logical_not(mid)))
    def _():
        pl.semaphore_wait(ready, 1)

    left_copy.start()

    @pl.when(jnp.logical_and(high_near, mid))
    def _():
        pl.semaphore_wait(barrier, half - 1)
        greet(ready, {"sub": 0})

    @pl.when(jnp.logical_and(high_far, mid))
    def _():
        pl.semaphore_wait(ready, 1)

    @pl.when(jnp.logical_not(low))
    def _():
        start(half, n_row, True)

    loads[7].wait()
    gating = jax.nn.sigmoid(
        jnp.dot(
            normed, w_v[:, 4 * hidden : 4 * hidden + chan], preferred_element_type=jnp.float32
        )
    ).astype(jnp.bfloat16)
    for load in loads[8:]:
        load.wait()

    @pl.when(low_far)
    def _():
        pl.semaphore_wait(barrier, half - 1)
        greet(ready, {"sub": 0})

    @pl.when(low_near)
    def _():
        pl.semaphore_wait(ready, 1)

    @pl.when(low)
    def _():
        start(half, n_row - 1, False)
        pl.semaphore_wait(late, 1)

    @pl.when(low_far)
    def _():
        greet(late, {"sub": 0})

    @pl.when(low)
    def _():
        copies[-1].start()

    left_copy.wait_recv()
    left_all = left_buf[...].astype(jnp.float32)
    for source in range(half):
        for source_sub in range(2):
            mine = jnp.logical_and(sub * half + source == row, sub == source_sub)

            @pl.when(jnp.logical_not(mine))
            def _():
                pltpu.make_async_remote_copy(
                    src_ref=right_send,
                    dst_ref=right_buf.at[source, source_sub],
                    send_sem=send_sem.at[0],
                    recv_sem=recv_sem.at[source, source_sub],
                    device_id={"sub": other},
                    device_id_type=pl.DeviceIdType.MESH,
                ).wait_recv()

    @pl.when(jnp.logical_and(low_far, row == 0))
    def _():
        raw = right_buf[half - 1].astype(jnp.float32).reshape(2 * rows * cols, chan)
        raw = layer_norm(raw, vec_v[0], vec_v[1], -1).astype(jnp.bfloat16)
        far = gated(raw, w_v[:, 0 : 2 * hidden])
        right_buf[half - 1] = far.reshape(2, rows, cols, hidden)

    for source in range(half):
        block = right_buf[source].astype(jnp.float32)
        for i in range(rows):
            prod = left_all[:, i][:, None] * block
            prod = prod[0] + prod[1]
            prod = jnp.sum(prod.reshape(rows, cols // 8, 8, hidden), axis=1)
            tri_v[i, source * rows : (source + 1) * rows, :] = jnp.sum(prod, axis=1)

    tri = tri_v[...].reshape(rows * cols, hidden).astype(jnp.bfloat16).astype(jnp.float32)
    hidden_normed = layer_norm(tri, vec_v[2], vec_v[3], -1).astype(jnp.bfloat16)
    mixed = jnp.dot(hidden_normed, wo_v[...], preferred_element_type=jnp.float32)
    out = (gating.astype(jnp.float32) * mixed).astype(jnp.bfloat16)
    out_ref[...] = out.reshape(rows, cols, chan)

    left_copy.wait_send()
    for q in range(n_row):

        @pl.when(sent[q])
        def _():
            copies[q].wait_send()


def one_round(n_row, pair_rep, norm_gain, norm_bias, *rest):
    w_a_proj, w_a_gate, w_b_proj, w_b_gate, w_gate, out_gain, out_bias, w_out = rest
    rows, cols, chan = pair_rep.shape
    hidden = w_a_proj.shape[1]
    half = n_row // 2
    hbm = pl.BlockSpec(memory_space=pltpu.HBM)
    return pl.pallas_call(
        functools.partial(kernel, n_row),
        out_shape=pltpu.VMEM((rows, cols, chan), jnp.bfloat16),
        in_specs=[hbm] * 11,
        out_specs=pl.BlockSpec(memory_space=pltpu.VMEM),
        scratch_shapes=[
            pltpu.VMEM((rows, cols, chan), jnp.bfloat16),
            pltpu.VMEM((4, 1, chan), jnp.float32),
            pltpu.VMEM((chan, 4 * hidden + chan), jnp.bfloat16),
            pltpu.VMEM((hidden, chan), jnp.bfloat16),
            pltpu.VMEM((rows, cols, hidden), jnp.bfloat16),
            pltpu.VMEM((half, 2, rows, cols, hidden), jnp.bfloat16),
            pltpu.VMEM((2, rows, cols, hidden), jnp.bfloat16),
            pltpu.VMEM((rows, cols, hidden), jnp.float32),
            pltpu.SemaphoreType.DMA((11,)),
            pltpu.SemaphoreType.DMA((n_row + 1,)),
            pltpu.SemaphoreType.DMA((half, 2)),
            pltpu.SemaphoreType.DMA,
            pltpu.SemaphoreType.REGULAR,
            pltpu.SemaphoreType.REGULAR,
        ],
        compiler_params=pltpu.CompilerParams(
            collective_id=0, has_side_effects=True, vmem_limit_bytes=16 * 2**20
        ),
    )(
        *(
            pltpu.with_memory_space_constraint(operand, pltpu.HBM)
            for operand in (
                pair_rep,
                norm_gain.reshape(1, chan),
                norm_bias.reshape(1, chan),
                w_a_proj,
                w_a_gate,
                w_b_proj,
                w_b_gate,
                w_gate,
                out_gain.reshape(1, hidden),
                out_bias.reshape(1, hidden),
                w_out,
            )
        )
    )


def body(n_row, n_sub, *operands):
    rows, cols, chan = operands[0].shape
    hidden = operands[3].shape[1]
    gathered = cols * cols * n_sub * hidden * 2
    if n_sub == 2 and n_row % 2 == 0 and cols % 16 == 0 and hidden == chan and gathered <= 4 * 2**20:
        return one_round(n_row, *operands)
    return per_device(*operands)


def solution(mesh):
    in_specs = (P(("grp", "row"), "sub", None), P(), P(), P(), P(), P(), P(), P(), P(), P(), P())
    out_specs = P(("grp", "row"), "sub", None)
    return jax.shard_map(
        functools.partial(body, mesh.shape["row"], mesh.shape["sub"]),
        mesh=mesh,
        in_specs=in_specs,
        out_specs=out_specs,
        check_vma=False,
    )
```

```python
import functools

import jax
import jax.numpy as jnp
from jax import lax
from jax.experimental import pallas as pl
from jax.experimental.pallas import tpu as pltpu
from jax.sharding import PartitionSpec as P

EPSILON = 1e-05


def layer_norm(values, gain, shift, axis):
    centred = values - jnp.mean(values, axis=axis, keepdims=True)
    variance = jnp.mean(centred * centred, axis=axis, keepdims=True)
    return centred * lax.rsqrt(variance + EPSILON) * gain + shift


def per_device(
    pair_rep,
    norm_gain,
    norm_bias,
    w_a_proj,
    w_a_gate,
    w_b_proj,
    w_b_gate,
    w_gate,
    out_gain,
    out_bias,
    w_out,
):
    hidden = w_a_proj.shape[1]
    w_inner = jnp.concatenate([w_a_proj, w_a_gate, w_b_proj, w_b_gate], axis=1)
    normed = layer_norm(pair_rep.astype(jnp.float32), norm_gain, norm_bias, -1).astype(jnp.bfloat16)
    inner = jnp.einsum("rkc,cm->mrk", normed, w_inner, preferred_element_type=jnp.float32)
    left_local = (jax.nn.sigmoid(inner[hidden : 2 * hidden]) * inner[:hidden]).astype(jnp.bfloat16)
    right_local = (
        jax.nn.sigmoid(inner[3 * hidden : 4 * hidden]) * inner[2 * hidden : 3 * hidden]
    ).astype(jnp.bfloat16)
    gating = jax.nn.sigmoid(
        jnp.einsum("rkc,cd->rkd", normed, w_gate, preferred_element_type=jnp.float32)
    ).astype(jnp.bfloat16)
    left_chan, right_chan = (
        lax.all_to_all(left_local, "row", split_axis=0, concat_axis=1, tiled=True),
        lax.all_to_all(right_local, "row", split_axis=0, concat_axis=1, tiled=True),
    )
    left_rows = lax.all_to_all(left_chan, "sub", split_axis=1, concat_axis=2, tiled=True)
    triangle = jnp.einsum(
        "hik,hjk->hij",
        left_rows,
        lax.all_gather(right_chan, "sub", axis=2, tiled=True),
        preferred_element_type=jnp.float32,
    ).astype(jnp.bfloat16)
    regrouped = lax.all_to_all(
        lax.all_to_all(triangle, "sub", split_axis=2, concat_axis=1, tiled=True),
        "row",
        split_axis=1,
        concat_axis=0,
        tiled=True,
    )
    hidden_normed = layer_norm(
        regrouped.astype(jnp.float32), out_gain[:, None, None], out_bias[:, None, None], 0
    ).astype(jnp.bfloat16)
    mixed = jnp.einsum("hrj,hc->rjc", hidden_normed, w_out, preferred_element_type=jnp.float32)
    return (gating.astype(jnp.float32) * mixed).astype(jnp.bfloat16)


def gated(normed, weights):
    hidden = weights.shape[1] // 2
    inner = jnp.dot(normed, weights, preferred_element_type=jnp.float32)
    return (jax.nn.sigmoid(inner[:, hidden:]) * inner[:, :hidden]).astype(jnp.bfloat16)


def kernel(
    n_row,
    pair_hbm,
    ngain_hbm,
    nbias_hbm,
    wap_hbm,
    wag_hbm,
    wbp_hbm,
    wbg_hbm,
    wg_hbm,
    ogain_hbm,
    obias_hbm,
    wo_hbm,
    out_ref,
    pair_v,
    vec_v,
    w_v,
    wo_v,
    right_send,
    right_buf,
    left_buf,
    tri_v,
    in_sem,
    send_sem,
    recv_sem,
    left_sem,
    ready,
    late,
):
    rows, cols, chan = pair_v.shape
    hidden = right_send.shape[-1]
    half = n_row // 2
    row = lax.axis_index("row")
    sub = lax.axis_index("sub")
    other = 1 - sub
    owner = row // half
    slot = lax.rem(row, half)
    near = sub == owner
    low = owner == 0
    low_near = jnp.logical_and(low, sub == 0)
    low_far = jnp.logical_and(low, sub == 1)
    high_near = jnp.logical_and(owner == 1, sub == 1)
    high_far = jnp.logical_and(owner == 1, sub == 0)
    last = row == n_row - 1
    split = half // 2
    mid = jnp.logical_and(owner == 1, slot < split)
    outer = jnp.logical_and(owner == 1, jnp.logical_and(slot >= split, jnp.logical_not(last)))

    loads = [
        pltpu.make_async_copy(pair_hbm, pair_v, in_sem.at[0]),
        pltpu.make_async_copy(ngain_hbm, vec_v.at[0], in_sem.at[1]),
        pltpu.make_async_copy(nbias_hbm, vec_v.at[1], in_sem.at[2]),
        pltpu.make_async_copy(wbp_hbm, w_v.at[:, 0:hidden], in_sem.at[3]),
        pltpu.make_async_copy(wbg_hbm, w_v.at[:, hidden : 2 * hidden], in_sem.at[4]),
        pltpu.make_async_copy(wap_hbm, w_v.at[:, 2 * hidden : 3 * hidden], in_sem.at[5]),
        pltpu.make_async_copy(wag_hbm, w_v.at[:, 3 * hidden : 4 * hidden], in_sem.at[6]),
        pltpu.make_async_copy(wg_hbm, w_v.at[:, 4 * hidden : 4 * hidden + chan], in_sem.at[7]),
        pltpu.make_async_copy(ogain_hbm, vec_v.at[2], in_sem.at[8]),
        pltpu.make_async_copy(obias_hbm, vec_v.at[3], in_sem.at[9]),
        pltpu.make_async_copy(wo_hbm, wo_v, in_sem.at[10]),
    ]
    barrier = pltpu.get_barrier_semaphore()

    def greet(semaphore, target):
        pl.semaphore_signal(
            semaphore, inc=1, device_id=target, device_id_type=pl.DeviceIdType.MESH
        )

    @pl.when(low_near)
    def _():
        for step in range(1, half):
            greet(barrier, {"row": lax.rem(slot + step, half), "sub": 0})

    @pl.when(low_far)
    def _():
        greet(barrier, {"sub": 0})
        for step in range(half)[::-1]:
            greet(barrier, {"row": half + step, "sub": 0})
            if step >= split:
                greet(barrier, {"row": half + step, "sub": 1})

    @pl.when(jnp.logical_and(high_far, jnp.logical_not(last)))
    def _():
        for step in range(half):
            greet(barrier, {"row": step, "sub": 1})

    @pl.when(high_near)
    def _():
        greet(barrier, {"sub": 0})
        for step in range(half):

            @pl.when(slot != step)
            def _():
                greet(barrier, {"row": half + step, "sub": 1})
                if step >= split:
                    greet(barrier, {"row": half + step, "sub": 0})

    left_copy = pltpu.make_async_remote_copy(
        src_ref=left_buf.at[sub],
        dst_ref=left_buf.at[sub],
        send_sem=send_sem.at[n_row],
        recv_sem=left_sem,
        device_id={"sub": other},
        device_id_type=pl.DeviceIdType.MESH,
    )

    def block_copy(source, index, target_row, target_sub):
        return pltpu.make_async_remote_copy(
            src_ref=source,
            dst_ref=right_buf.at[slot, sub],
            send_sem=send_sem.at[index],
            recv_sem=recv_sem.at[slot, sub],
            device_id={"row": target_row, "sub": target_sub},
            device_id_type=pl.DeviceIdType.MESH,
        )

    raw_copy = block_copy(pair_hbm, 0, 0, owner)
    copies = [block_copy(right_send, q, q, owner) for q in range(n_row)]
    copies[half:] = [
        block_copy(right_send, q, q, jnp.where(low, 0, 1)) for q in range(half, n_row)
    ]
    sent = [jnp.logical_not(jnp.logical_and(near, row == q)) for q in range(n_row)]

    def start(first, end, guarded):
        for q in range(first, end):
            if guarded:

                @pl.when(sent[q])
                def _():
                    copies[q].start()
            else:
                copies[q].start()

    @pl.when(last)
    def _():
        pl.semaphore_wait(barrier, 2 * half - sub)
        raw_copy.start()

        @pl.when(sub == 0)
        def _():
            greet(ready, {"sub": 1})
            for step in range(half):
                greet(late, {"row": step, "sub": 1})

    for load in loads:
        load.start()

    @pl.when(low_near)
    def _():
        pl.semaphore_wait(barrier, half)
        greet(ready, {"sub": 1})

    @pl.when(jnp.logical_and(high_far, mid))
    def _():
        pl.semaphore_wait(barrier, half + 1)
        greet(ready, {"sub": 1})

    for load in loads[:3]:
        load.wait()
    pair = pair_v[...].astype(jnp.float32).reshape(rows * cols, chan)
    normed = layer_norm(pair, vec_v[0], vec_v[1], -1).astype(jnp.bfloat16)
    for load in loads[3:5]:
        load.wait()
    right = gated(normed, w_v[:, 0 : 2 * hidden]).reshape(rows, cols, hidden)
    right_send[...] = right

    @pl.when(low_far)
    def _():
        pl.semaphore_wait(ready, 1)

    @pl.when(jnp.logical_and(high_near, mid))
    def _():
        pl.semaphore_wait(ready, 1)

    @pl.when(outer)
    def _():
        pl.semaphore_wait(barrier, 2 * half - sub)

        @pl.when(sub == 0)
        def _():
            greet(ready, {"sub": 1})

    @pl.when(jnp.logical_and(sent[0], jnp.logical_not(last)))
    def _():
        copies[0].start()

    start(1, half, True)

    @pl.when(near)
    def _():
        right_buf[slot, sub] = right

    for load in loads[5:7]:
        load.wait()
    left = gated(normed, w_v[:, 2 * hidden : 4 * hidden])
    left_buf[sub] = left.reshape(rows, cols, hidden)

    @pl.when(jnp.logical_and(high_near, jnp.logical_not(mid)))
    def _():
        pl.semaphore_wait(ready, 1)

    left_copy.start()

    @pl.when(jnp.logical_and(high_near, mid))
    def _():
        pl.semaphore_wait(barrier, half - 1)
        greet(ready, {"sub": 0})

    @pl.when(jnp.logical_and(high_far, mid))
    def _():
        pl.semaphore_wait(ready, 1)

    @pl.when(jnp.logical_not(low))
    def _():
        start(half, n_row, True)

    loads[7].wait()
    gating = jax.nn.sigmoid(
        jnp.dot(
            normed, w_v[:, 4 * hidden : 4 * hidden + chan], preferred_element_type=jnp.float32
        )
    ).astype(jnp.bfloat16)
    for load in loads[8:]:
        load.wait()

    @pl.when(low_far)
    def _():
        pl.semaphore_wait(barrier, half - 1)
        greet(ready, {"sub": 0})

    @pl.when(low_near)
    def _():
        pl.semaphore_wait(ready, 1)

    @pl.when(low)
    def _():
        start(half, n_row - 1, False)
        pl.semaphore_wait(late, 1)

    @pl.when(low_far)
    def _():
        greet(late, {"sub": 0})

    @pl.when(low)
    def _():
        copies[-1].start()

    left_copy.wait_recv()
    left_all = left_buf[...].astype(jnp.float32)
    for source in range(half):
        for source_sub in range(2):
            mine = jnp.logical_and(sub * half + source == row, sub == source_sub)

            @pl.when(jnp.logical_not(mine))
            def _():
                pltpu.make_async_remote_copy(
                    src_ref=right_send,
                    dst_ref=right_buf.at[source, source_sub],
                    send_sem=send_sem.at[0],
                    recv_sem=recv_sem.at[source, source_sub],
                    device_id={"sub": other},
                    device_id_type=pl.DeviceIdType.MESH,
                ).wait_recv()

    @pl.when(jnp.logical_and(low_far, row == 0))
    def _():
        raw = right_buf[half - 1].astype(jnp.float32).reshape(2 * rows * cols, chan)
        raw = layer_norm(raw, vec_v[0], vec_v[1], -1).astype(jnp.bfloat16)
        far = gated(raw, w_v[:, 0 : 2 * hidden])
        right_buf[half - 1] = far.reshape(2, rows, cols, hidden)

    for source in range(half):
        block = right_buf[source].astype(jnp.float32)
        for i in range(rows):
            prod = left_all[:, i][:, None] * block
            prod = prod[0] + prod[1]
            prod = jnp.sum(prod.reshape(rows, cols // 8, 8, hidden), axis=1)
            tri_v[i, source * rows : (source + 1) * rows, :] = jnp.sum(prod, axis=1)

    tri = tri_v[...].reshape(rows * cols, hidden).astype(jnp.bfloat16).astype(jnp.float32)
    hidden_normed = layer_norm(tri, vec_v[2], vec_v[3], -1).astype(jnp.bfloat16)
    mixed = jnp.dot(hidden_normed, wo_v[...], preferred_element_type=jnp.float32)
    out = (gating.astype(jnp.float32) * mixed).astype(jnp.bfloat16)
    out_ref[...] = out.reshape(rows, cols, chan)

    left_copy.wait_send()
    for q in range(n_row):

        @pl.when(sent[q])
        def _():
            copies[q].wait_send()


def one_round(n_row, pair_rep, norm_gain, norm_bias, *rest):
    w_a_proj, w_a_gate, w_b_proj, w_b_gate, w_gate, out_gain, out_bias, w_out = rest
    rows, cols, chan = pair_rep.shape
    hidden = w_a_proj.shape[1]
    half = n_row // 2
    hbm = pl.BlockSpec(memory_space=pltpu.HBM)
    return pl.pallas_call(
        functools.partial(kernel, n_row),
        out_shape=pltpu.VMEM((rows, cols, chan), jnp.bfloat16),
        in_specs=[hbm] * 11,
        out_specs=pl.BlockSpec(memory_space=pltpu.VMEM),
        scratch_shapes=[
            pltpu.VMEM((rows, cols, chan), jnp.bfloat16),
            pltpu.VMEM((4, 1, chan), jnp.float32),
            pltpu.VMEM((chan, 4 * hidden + chan), jnp.bfloat16),
            pltpu.VMEM((hidden, chan), jnp.bfloat16),
            pltpu.VMEM((rows, cols, hidden), jnp.bfloat16),
            pltpu.VMEM((half, 2, rows, cols, hidden), jnp.bfloat16),
            pltpu.VMEM((2, rows, cols, hidden), jnp.bfloat16),
            pltpu.VMEM((rows, cols, hidden), jnp.float32),
            pltpu.SemaphoreType.DMA((11,)),
            pltpu.SemaphoreType.DMA((n_row + 1,)),
            pltpu.SemaphoreType.DMA((half, 2)),
            pltpu.SemaphoreType.DMA,
            pltpu.SemaphoreType.REGULAR,
            pltpu.SemaphoreType.REGULAR,
        ],
        compiler_params=pltpu.CompilerParams(
            collective_id=0, has_side_effects=True, vmem_limit_bytes=16 * 2**20
        ),
    )(
        *(
            pltpu.with_memory_space_constraint(operand, pltpu.HBM)
            for operand in (
                pair_rep,
                norm_gain.reshape(1, chan),
                norm_bias.reshape(1, chan),
                w_a_proj,
                w_a_gate,
                w_b_proj,
                w_b_gate,
                w_gate,
                out_gain.reshape(1, hidden),
                out_bias.reshape(1, hidden),
                w_out,
            )
        )
    )


def body(n_row, n_sub, *operands):
    rows, cols, chan = operands[0].shape
    hidden = operands[3].shape[1]
    gathered = cols * cols * n_sub * hidden * 2
    if n_sub == 2 and n_row % 2 == 0 and cols % 16 == 0 and hidden == chan and gathered <= 4 * 2**20:
        return one_round(n_row, *operands)
    return per_device(*operands)


def solution(mesh):
    in_specs = (P(("grp", "row"), "sub", None), P(), P(), P(), P(), P(), P(), P(), P(), P(), P())
    out_specs = P(("grp", "row"), "sub", None)
    return jax.shard_map(
        functools.partial(body, mesh.shape["row"], mesh.shape["sub"]),
        mesh=mesh,
        in_specs=in_specs,
        out_specs=out_specs,
        check_vma=False,
    )
```

```python
import functools

import jax
import jax.numpy as jnp
from jax import lax
from jax.experimental import pallas as pl
from jax.experimental.pallas import tpu as pltpu
from jax.sharding import PartitionSpec as P

EPSILON = 1e-05


def layer_norm(values, gain, shift, axis):
    centred = values - jnp.mean(values, axis=axis, keepdims=True)
    variance = jnp.mean(centred * centred, axis=axis, keepdims=True)
    return centred * lax.rsqrt(variance + EPSILON) * gain + shift


def per_device(
    pair_rep,
    norm_gain,
    norm_bias,
    w_a_proj,
    w_a_gate,
    w_b_proj,
    w_b_gate,
    w_gate,
    out_gain,
    out_bias,
    w_out,
):
    hidden = w_a_proj.shape[1]
    w_inner = jnp.concatenate([w_a_proj, w_a_gate, w_b_proj, w_b_gate], axis=1)
    normed = layer_norm(pair_rep.astype(jnp.float32), norm_gain, norm_bias, -1).astype(jnp.bfloat16)
    inner = jnp.einsum("rkc,cm->mrk", normed, w_inner, preferred_element_type=jnp.float32)
    left_local = (jax.nn.sigmoid(inner[hidden : 2 * hidden]) * inner[:hidden]).astype(jnp.bfloat16)
    right_local = (
        jax.nn.sigmoid(inner[3 * hidden : 4 * hidden]) * inner[2 * hidden : 3 * hidden]
    ).astype(jnp.bfloat16)
    gating = jax.nn.sigmoid(
        jnp.einsum("rkc,cd->rkd", normed, w_gate, preferred_element_type=jnp.float32)
    ).astype(jnp.bfloat16)
    left_chan, right_chan = (
        lax.all_to_all(left_local, "row", split_axis=0, concat_axis=1, tiled=True),
        lax.all_to_all(right_local, "row", split_axis=0, concat_axis=1, tiled=True),
    )
    left_rows = lax.all_to_all(left_chan, "sub", split_axis=1, concat_axis=2, tiled=True)
    triangle = jnp.einsum(
        "hik,hjk->hij",
        left_rows,
        lax.all_gather(right_chan, "sub", axis=2, tiled=True),
        preferred_element_type=jnp.float32,
    ).astype(jnp.bfloat16)
    regrouped = lax.all_to_all(
        lax.all_to_all(triangle, "sub", split_axis=2, concat_axis=1, tiled=True),
        "row",
        split_axis=1,
        concat_axis=0,
        tiled=True,
    )
    hidden_normed = layer_norm(
        regrouped.astype(jnp.float32), out_gain[:, None, None], out_bias[:, None, None], 0
    ).astype(jnp.bfloat16)
    mixed = jnp.einsum("hrj,hc->rjc", hidden_normed, w_out, preferred_element_type=jnp.float32)
    return (gating.astype(jnp.float32) * mixed).astype(jnp.bfloat16)


def sigmoid(values):
    return 0.5 * jnp.tanh(0.5 * values) + 0.5


def centre(values, gain):
    centred = values - jnp.mean(values, axis=-1, keepdims=True)
    scale = lax.rsqrt(jnp.mean(centred * centred, axis=-1, keepdims=True) + EPSILON)
    return (centred * gain).astype(jnp.bfloat16), scale


def through(shift, weights):
    high = shift.astype(jnp.bfloat16)
    low = (shift - high.astype(jnp.float32)).astype(jnp.bfloat16)
    pair = jnp.concatenate([jnp.broadcast_to(high, (8, high.shape[1])), jnp.broadcast_to(low, (8, low.shape[1]))], axis=0)
    mixed = jnp.dot(pair, weights, preferred_element_type=jnp.float32)
    return mixed[0:1] + mixed[8:9]


def gated(centred, scale, shift, weights):
    hidden = weights.shape[1] // 2
    inner = jnp.dot(centred, weights, preferred_element_type=jnp.float32) * scale + shift
    return (sigmoid(inner[:, hidden:]) * inner[:, :hidden]).astype(jnp.bfloat16)


def kernel(
    n_row,
    pair_hbm,
    ngain_hbm,
    nbias_hbm,
    wap_hbm,
    wag_hbm,
    wbp_hbm,
    wbg_hbm,
    wg_hbm,
    ogain_hbm,
    obias_hbm,
    wo_hbm,
    out_ref,
    pair_v,
    vec_v,
    w_v,
    wo_v,
    right_send,
    right_buf,
    left_buf,
    tri_v,
    in_sem,
    send_sem,
    recv_sem,
    left_sem,
    ready,
    late,
):
    rows, cols, chan = pair_v.shape
    hidden = right_send.shape[-1]
    half = n_row // 2
    row = lax.axis_index("row")
    sub = lax.axis_index("sub")
    other = 1 - sub
    owner = row // half
    slot = lax.rem(row, half)
    near = sub == owner
    low = owner == 0
    low_near = jnp.logical_and(low, sub == 0)
    low_far = jnp.logical_and(low, sub == 1)
    high_near = jnp.logical_and(owner == 1, sub == 1)
    high_far = jnp.logical_and(owner == 1, sub == 0)
    last = row == n_row - 1
    split = half // 2
    order = [half + q for pair in zip(range(split), range(split, half - 1)) for q in pair]
    order += [q for q in range(half, n_row - 1) if q not in order]
    mid = jnp.logical_and(owner == 1, slot < split)
    outer = jnp.logical_and(owner == 1, jnp.logical_and(slot >= split, jnp.logical_not(last)))

    loads = [
        pltpu.make_async_copy(pair_hbm, pair_v, in_sem.at[0]),
        pltpu.make_async_copy(ngain_hbm, vec_v.at[0], in_sem.at[1]),
        pltpu.make_async_copy(nbias_hbm, vec_v.at[1], in_sem.at[2]),
        pltpu.make_async_copy(wbp_hbm, w_v.at[:, 0:hidden], in_sem.at[3]),
        pltpu.make_async_copy(wbg_hbm, w_v.at[:, hidden : 2 * hidden], in_sem.at[4]),
        pltpu.make_async_copy(wap_hbm, w_v.at[:, 2 * hidden : 3 * hidden], in_sem.at[5]),
        pltpu.make_async_copy(wag_hbm, w_v.at[:, 3 * hidden : 4 * hidden], in_sem.at[6]),
        pltpu.make_async_copy(wg_hbm, w_v.at[:, 4 * hidden : 4 * hidden + chan], in_sem.at[7]),
        pltpu.make_async_copy(ogain_hbm, vec_v.at[2], in_sem.at[8]),
        pltpu.make_async_copy(obias_hbm, vec_v.at[3], in_sem.at[9]),
        pltpu.make_async_copy(wo_hbm, wo_v, in_sem.at[10]),
    ]
    barrier = pltpu.get_barrier_semaphore()

    def greet(semaphore, target):
        pl.semaphore_signal(
            semaphore, inc=1, device_id=target, device_id_type=pl.DeviceIdType.MESH
        )

    @pl.when(low_near)
    def _():
        for step in range(1, half):
            greet(barrier, {"row": lax.rem(slot + step, half), "sub": 0})

    @pl.when(low_far)
    def _():
        greet(barrier, {"sub": 0})
        for step in range(half)[::-1]:
            greet(barrier, {"row": half + step, "sub": 0})
            if step >= split:
                greet(barrier, {"row": half + step, "sub": 1})

    @pl.when(jnp.logical_and(high_far, jnp.logical_not(last)))
    def _():
        for step in range(half):
            greet(barrier, {"row": step, "sub": 1})

    @pl.when(high_near)
    def _():
        greet(barrier, {"sub": 0})
        for step in range(half):

            @pl.when(slot != step)
            def _():
                greet(barrier, {"row": half + step, "sub": 1})
                if step >= split:
                    greet(barrier, {"row": half + step, "sub": 0})

    left_copy = pltpu.make_async_remote_copy(
        src_ref=left_buf.at[sub],
        dst_ref=left_buf.at[sub],
        send_sem=send_sem.at[n_row],
        recv_sem=left_sem,
        device_id={"sub": other},
        device_id_type=pl.DeviceIdType.MESH,
    )

    def block_copy(source, index, target_row, target_sub):
        return pltpu.make_async_remote_copy(
            src_ref=source,
            dst_ref=right_buf.at[slot, sub],
            send_sem=send_sem.at[index],
            recv_sem=recv_sem.at[slot, sub],
            device_id={"row": target_row, "sub": target_sub},
            device_id_type=pl.DeviceIdType.MESH,
        )

    raw_copy = block_copy(pair_hbm, 0, 0, owner)
    copies = [block_copy(right_send, q, q, owner) for q in range(n_row)]
    sent = [jnp.logical_not(jnp.logical_and(near, row == q)) for q in range(n_row)]

    def start(first, end, guarded):
        for q in range(first, end):
            if guarded:

                @pl.when(sent[q])
                def _():
                    copies[q].start()
            else:
                copies[q].start()

    @pl.when(last)
    def _():
        pl.semaphore_wait(barrier, 2 * half - sub)
        raw_copy.start()

        @pl.when(sub == 0)
        def _():
            greet(ready, {"sub": 1})
            for step in range(half):
                greet(late, {"row": step, "sub": 1})

    for load in loads:
        load.start()

    @pl.when(low_near)
    def _():
        pl.semaphore_wait(barrier, half)
        greet(ready, {"sub": 1})

    @pl.when(jnp.logical_and(high_far, mid))
    def _():
        pl.semaphore_wait(barrier, half + 1)
        greet(ready, {"sub": 1})

    for load in loads[:3]:
        load.wait()
    pair = pair_v[...].astype(jnp.float32).reshape(rows * cols, chan)
    centred, scale = centre(pair, vec_v[0])
    for load in loads[3:5]:
        load.wait()
    right_shift = through(vec_v[1], w_v[:, 0 : 2 * hidden])
    right = gated(centred, scale, right_shift, w_v[:, 0 : 2 * hidden])
    right = right.reshape(rows, cols, hidden)
    right_send[...] = right

    @pl.when(low_far)
    def _():
        pl.semaphore_wait(ready, 1)

    @pl.when(jnp.logical_and(high_near, mid))
    def _():
        pl.semaphore_wait(ready, 1)

    @pl.when(outer)
    def _():
        pl.semaphore_wait(barrier, 2 * half - sub)

        @pl.when(sub == 0)
        def _():
            greet(ready, {"sub": 1})

    @pl.when(jnp.logical_and(sent[0], jnp.logical_not(last)))
    def _():
        copies[0].start()

    start(1, half, True)

    @pl.when(near)
    def _():
        right_buf[slot, sub] = right

    for load in loads[5:7]:
        load.wait()
    left_shift = through(vec_v[1], w_v[:, 2 * hidden : 4 * hidden])
    left = gated(centred, scale, left_shift, w_v[:, 2 * hidden : 4 * hidden])
    left_buf[sub] = left.reshape(rows, cols, hidden)

    @pl.when(jnp.logical_and(high_near, jnp.logical_not(mid)))
    def _():
        pl.semaphore_wait(ready, 1)

    left_copy.start()

    @pl.when(jnp.logical_and(high_near, mid))
    def _():
        pl.semaphore_wait(barrier, half - 1)
        greet(ready, {"sub": 0})

    @pl.when(jnp.logical_and(high_far, mid))
    def _():
        pl.semaphore_wait(ready, 1)

    @pl.when(jnp.logical_not(low))
    def _():
        start(half, n_row, True)

    loads[7].wait()
    gate = w_v[:, 4 * hidden : 4 * hidden + chan]
    gating = jnp.dot(centred, gate, preferred_element_type=jnp.float32) * scale
    gating = sigmoid(gating + through(vec_v[1], gate)).astype(jnp.bfloat16)
    for load in loads[8:]:
        load.wait()
    out_shift = through(vec_v[3], wo_v[...])

    @pl.when(low_far)
    def _():
        pl.semaphore_wait(barrier, half - 1)
        greet(ready, {"sub": 0})

    @pl.when(low_near)
    def _():
        pl.semaphore_wait(ready, 1)

    @pl.when(low)
    def _():
        for q in order:
            copies[q].start()
        pl.semaphore_wait(late, 1)

    @pl.when(low_far)
    def _():
        greet(late, {"sub": 0})

    @pl.when(low)
    def _():
        copies[-1].start()

    left_copy.wait_recv()

    def arrive(source, source_sub):
        return pltpu.make_async_remote_copy(
            src_ref=right_send,
            dst_ref=right_buf.at[source, source_sub],
            send_sem=send_sem.at[0],
            recv_sem=recv_sem.at[source, source_sub],
            device_id={"sub": other},
            device_id_type=pl.DeviceIdType.MESH,
        )

    def absorb(source, block):
        for i in range(rows):
            prod = left_buf[:, i].astype(jnp.float32)[:, None] * block
            prod = prod[0] + prod[1]
            prod = jnp.sum(prod.reshape(rows, cols // 8, 8, hidden), axis=1)
            tri_v[i, source * rows : (source + 1) * rows, :] = jnp.sum(prod, axis=1)

    def project(source):
        raw = right_buf[source].astype(jnp.float32).reshape(2 * rows * cols, chan)
        raw_centred, raw_scale = centre(raw, vec_v[0])
        far = gated(raw_centred, raw_scale, right_shift, w_v[:, 0 : 2 * hidden])
        return far.astype(jnp.float32).reshape(2, rows, cols, hidden)

    first = jnp.logical_and(low_far, row == 0)

    @pl.when(first)
    def _():
        for group in [list(range(half // 2)), list(range(half // 2, half))]:
            for source in group:
                for source_sub in range(2):
                    arrive(source, source_sub).wait_recv()
            for source in group[::-1]:
                if source == half - 1:
                    absorb(source, project(source))
                else:
                    absorb(source, right_buf[source].astype(jnp.float32))

    @pl.when(jnp.logical_not(first))
    def _():
        for group in [list(range(half // 2)), list(range(half // 2, half))]:
            for source in group:
                for source_sub in range(2):
                    mine = jnp.logical_and(sub * half + source == row, sub == source_sub)

                    @pl.when(jnp.logical_not(mine))
                    def _():
                        arrive(source, source_sub).wait_recv()

            for source in group:
                absorb(source, right_buf[source].astype(jnp.float32))

    tri = tri_v[...].reshape(rows * cols, hidden).astype(jnp.bfloat16).astype(jnp.float32)
    tri_centred, tri_scale = centre(tri, vec_v[2])
    mixed = jnp.dot(tri_centred, wo_v[...], preferred_element_type=jnp.float32)
    mixed = mixed * tri_scale + out_shift
    out = (gating.astype(jnp.float32) * mixed).astype(jnp.bfloat16)
    out_ref[...] = out.reshape(rows, cols, chan)

    left_copy.wait_send()
    for q in range(n_row):

        @pl.when(sent[q])
        def _():
            copies[q].wait_send()


def one_round(n_row, pair_rep, norm_gain, norm_bias, *rest):
    w_a_proj, w_a_gate, w_b_proj, w_b_gate, w_gate, out_gain, out_bias, w_out = rest
    rows, cols, chan = pair_rep.shape
    hidden = w_a_proj.shape[1]
    half = n_row // 2
    hbm = pl.BlockSpec(memory_space=pltpu.HBM)
    return pl.pallas_call(
        functools.partial(kernel, n_row),
        out_shape=pltpu.VMEM((rows, cols, chan), jnp.bfloat16),
        in_specs=[hbm] * 11,
        out_specs=pl.BlockSpec(memory_space=pltpu.VMEM),
        scratch_shapes=[
            pltpu.VMEM((rows, cols, chan), jnp.bfloat16),
            pltpu.VMEM((4, 1, chan), jnp.float32),
            pltpu.VMEM((chan, 4 * hidden + chan), jnp.bfloat16),
            pltpu.VMEM((hidden, chan), jnp.bfloat16),
            pltpu.VMEM((rows, cols, hidden), jnp.bfloat16),
            pltpu.VMEM((half, 2, rows, cols, hidden), jnp.bfloat16),
            pltpu.VMEM((2, rows, cols, hidden), jnp.bfloat16),
            pltpu.VMEM((rows, cols, hidden), jnp.float32),
            pltpu.SemaphoreType.DMA((11,)),
            pltpu.SemaphoreType.DMA((n_row + 1,)),
            pltpu.SemaphoreType.DMA((half, 2)),
            pltpu.SemaphoreType.DMA,
            pltpu.SemaphoreType.REGULAR,
            pltpu.SemaphoreType.REGULAR,
        ],
        compiler_params=pltpu.CompilerParams(
            collective_id=0, has_side_effects=True, vmem_limit_bytes=16 * 2**20
        ),
    )(
        *(
            pltpu.with_memory_space_constraint(operand, pltpu.HBM)
            for operand in (
                pair_rep,
                norm_gain.reshape(1, chan),
                norm_bias.reshape(1, chan),
                w_a_proj,
                w_a_gate,
                w_b_proj,
                w_b_gate,
                w_gate,
                out_gain.reshape(1, hidden),
                out_bias.reshape(1, hidden),
                w_out,
            )
        )
    )


def body(n_row, n_sub, *operands):
    rows, cols, chan = operands[0].shape
    hidden = operands[3].shape[1]
    gathered = cols * cols * n_sub * hidden * 2
    if n_sub == 2 and n_row % 2 == 0 and cols % 16 == 0 and hidden == chan and gathered <= 4 * 2**20:
        return one_round(n_row, *operands)
    return per_device(*operands)


def solution(mesh):
    in_specs = (P(("grp", "row"), "sub", None), P(), P(), P(), P(), P(), P(), P(), P(), P(), P())
    out_specs = P(("grp", "row"), "sub", None)
    return jax.shard_map(
        functools.partial(body, mesh.shape["row"], mesh.shape["sub"]),
        mesh=mesh,
        in_specs=in_specs,
        out_specs=out_specs,
        check_vma=False,
    )
```

```python
import functools

import jax
import jax.numpy as jnp
from jax import lax
from jax.experimental import pallas as pl
from jax.experimental.pallas import tpu as pltpu
from jax.sharding import PartitionSpec as P

EPSILON = 1e-05


def layer_norm(values, gain, shift, axis):
    centred = values - jnp.mean(values, axis=axis, keepdims=True)
    variance = jnp.mean(centred * centred, axis=axis, keepdims=True)
    return centred * lax.rsqrt(variance + EPSILON) * gain + shift


def per_device(
    pair_rep,
    norm_gain,
    norm_bias,
    w_a_proj,
    w_a_gate,
    w_b_proj,
    w_b_gate,
    w_gate,
    out_gain,
    out_bias,
    w_out,
):
    hidden = w_a_proj.shape[1]
    w_inner = jnp.concatenate([w_a_proj, w_a_gate, w_b_proj, w_b_gate], axis=1)
    normed = layer_norm(pair_rep.astype(jnp.float32), norm_gain, norm_bias, -1).astype(jnp.bfloat16)
    inner = jnp.einsum("rkc,cm->mrk", normed, w_inner, preferred_element_type=jnp.float32)
    left_local = (jax.nn.sigmoid(inner[hidden : 2 * hidden]) * inner[:hidden]).astype(jnp.bfloat16)
    right_local = (
        jax.nn.sigmoid(inner[3 * hidden : 4 * hidden]) * inner[2 * hidden : 3 * hidden]
    ).astype(jnp.bfloat16)
    gating = jax.nn.sigmoid(
        jnp.einsum("rkc,cd->rkd", normed, w_gate, preferred_element_type=jnp.float32)
    ).astype(jnp.bfloat16)
    left_chan, right_chan = (
        lax.all_to_all(left_local, "row", split_axis=0, concat_axis=1, tiled=True),
        lax.all_to_all(right_local, "row", split_axis=0, concat_axis=1, tiled=True),
    )
    left_rows = lax.all_to_all(left_chan, "sub", split_axis=1, concat_axis=2, tiled=True)
    triangle = jnp.einsum(
        "hik,hjk->hij",
        left_rows,
        lax.all_gather(right_chan, "sub", axis=2, tiled=True),
        preferred_element_type=jnp.float32,
    ).astype(jnp.bfloat16)
    regrouped = lax.all_to_all(
        lax.all_to_all(triangle, "sub", split_axis=2, concat_axis=1, tiled=True),
        "row",
        split_axis=1,
        concat_axis=0,
        tiled=True,
    )
    hidden_normed = layer_norm(
        regrouped.astype(jnp.float32), out_gain[:, None, None], out_bias[:, None, None], 0
    ).astype(jnp.bfloat16)
    mixed = jnp.einsum("hrj,hc->rjc", hidden_normed, w_out, preferred_element_type=jnp.float32)
    return (gating.astype(jnp.float32) * mixed).astype(jnp.bfloat16)


def sigmoid(values):
    return 0.5 * jnp.tanh(0.5 * values) + 0.5


def centre(values, gain):
    centred = values - jnp.mean(values, axis=-1, keepdims=True)
    scale = lax.rsqrt(jnp.mean(centred * centred, axis=-1, keepdims=True) + EPSILON)
    return (centred * gain).astype(jnp.bfloat16), scale


def through(shift, weights):
    high = shift.astype(jnp.bfloat16)
    low = (shift - high.astype(jnp.float32)).astype(jnp.bfloat16)
    pair = jnp.concatenate([jnp.broadcast_to(high, (8, high.shape[1])), jnp.broadcast_to(low, (8, low.shape[1]))], axis=0)
    mixed = jnp.dot(pair, weights, preferred_element_type=jnp.float32)
    return mixed[0:1] + mixed[8:9]


def gated(centred, scale, shift, weights):
    hidden = weights.shape[1] // 2
    inner = jnp.dot(centred, weights, preferred_element_type=jnp.float32) * scale + shift
    return (sigmoid(inner[:, hidden:]) * inner[:, :hidden]).astype(jnp.bfloat16)


def kernel(
    n_row,
    pair_hbm,
    ngain_hbm,
    nbias_hbm,
    wap_hbm,
    wag_hbm,
    wbp_hbm,
    wbg_hbm,
    wg_hbm,
    ogain_hbm,
    obias_hbm,
    wo_hbm,
    out_ref,
    pair_v,
    vec_v,
    w_v,
    right_send,
    right_buf,
    left_buf,
    tri_v,
    in_sem,
    send_sem,
    recv_sem,
    left_sem,
    ready,
    late,
):
    rows, cols, chan = pair_v.shape
    hidden = right_send.shape[-1]
    half = n_row // 2
    row = lax.axis_index("row")
    sub = lax.axis_index("sub")
    other = 1 - sub
    owner = row // half
    slot = lax.rem(row, half)
    near = sub == owner
    low = owner == 0
    low_near = jnp.logical_and(low, sub == 0)
    low_far = jnp.logical_and(low, sub == 1)
    high_near = jnp.logical_and(owner == 1, sub == 1)
    high_far = jnp.logical_and(owner == 1, sub == 0)
    last = row == n_row - 1
    split = half // 2
    order = [half + q for pair in zip(range(split), range(split, half - 1)) for q in pair]
    order += [q for q in range(half, n_row - 1) if q not in order]
    mid = jnp.logical_and(owner == 1, slot < split)
    outer = jnp.logical_and(owner == 1, jnp.logical_and(slot >= split, jnp.logical_not(last)))

    weights = (wbp_hbm, wbg_hbm, wap_hbm, wag_hbm, wg_hbm, wo_hbm)
    loads = [pltpu.make_async_copy(pair_hbm, pair_v, in_sem.at[0])]
    for n, vector in enumerate((ngain_hbm, nbias_hbm, ogain_hbm, obias_hbm)):
        loads.append(pltpu.make_async_copy(vector, vec_v.at[n], in_sem.at[1]))
    for n, weight in enumerate(weights):
        span = w_v.at[:, n * hidden : (n + 1) * hidden]
        loads.append(pltpu.make_async_copy(weight, span, in_sem.at[2 if n < 2 else 3]))

    def loaded(span, index):
        pltpu.make_async_copy(span, span, in_sem.at[index]).wait()

    barrier = pltpu.get_barrier_semaphore()

    def greet(semaphore, target):
        pl.semaphore_signal(
            semaphore, inc=1, device_id=target, device_id_type=pl.DeviceIdType.MESH
        )

    @pl.when(low_near)
    def _():
        for step in range(1, half):
            greet(barrier, {"row": lax.rem(slot + step, half), "sub": 0})

    @pl.when(low_far)
    def _():
        greet(barrier, {"sub": 0})
        for step in range(half)[::-1]:
            greet(barrier, {"row": half + step, "sub": 0})
            if step >= split:
                greet(barrier, {"row": half + step, "sub": 1})

    @pl.when(jnp.logical_and(high_far, jnp.logical_not(last)))
    def _():
        for step in range(half):
            greet(barrier, {"row": step, "sub": 1})

    @pl.when(high_near)
    def _():
        greet(barrier, {"sub": 0})
        for step in range(half):

            @pl.when(slot != step)
            def _():
                greet(barrier, {"row": half + step, "sub": 1})
                if step >= split:
                    greet(barrier, {"row": half + step, "sub": 0})

    left_copy = pltpu.make_async_remote_copy(
        src_ref=left_buf.at[sub],
        dst_ref=left_buf.at[sub],
        send_sem=send_sem.at[1],
        recv_sem=left_sem,
        device_id={"sub": other},
        device_id_type=pl.DeviceIdType.MESH,
    )

    def block_copy(source, target_row, target_sub):
        return pltpu.make_async_remote_copy(
            src_ref=source,
            dst_ref=right_buf.at[2 * slot + sub],
            send_sem=send_sem.at[0],
            recv_sem=recv_sem.at[slot // split],
            device_id={"row": target_row, "sub": target_sub},
            device_id_type=pl.DeviceIdType.MESH,
        )

    raw_copy = block_copy(pair_hbm, 0, owner)
    copies = [block_copy(right_send, q, owner) for q in range(n_row)]
    sent = [jnp.logical_not(jnp.logical_and(near, row == q)) for q in range(n_row)]

    def start(first, end, guarded):
        for q in range(first, end):
            if guarded:

                @pl.when(sent[q])
                def _():
                    copies[q].start()
            else:
                copies[q].start()

    @pl.when(last)
    def _():
        pl.semaphore_wait(barrier, 2 * half - sub)
        raw_copy.start()

        @pl.when(sub == 0)
        def _():
            greet(ready, {"sub": 1})
            for step in range(half):
                greet(late, {"row": step, "sub": 1})

    for load in loads:
        load.start()

    @pl.when(low_near)
    def _():
        pl.semaphore_wait(barrier, half)
        greet(ready, {"sub": 1})

    @pl.when(jnp.logical_and(high_far, mid))
    def _():
        pl.semaphore_wait(barrier, half + 1)
        greet(ready, {"sub": 1})

    loaded(pair_v, 0)
    loaded(vec_v, 1)
    pair = pair_v[...].astype(jnp.float32).reshape(rows * cols, chan)
    centred, scale = centre(pair, vec_v[0])
    loaded(w_v.at[:, 0 : 2 * hidden], 2)
    right_shift = through(vec_v[1], w_v[:, 0 : 2 * hidden])
    right = gated(centred, scale, right_shift, w_v[:, 0 : 2 * hidden])
    right = right.reshape(rows, cols, hidden)
    right_send[...] = right

    @pl.when(low_far)
    def _():
        pl.semaphore_wait(ready, 1)

    @pl.when(jnp.logical_and(high_near, mid))
    def _():
        pl.semaphore_wait(ready, 1)

    @pl.when(outer)
    def _():
        pl.semaphore_wait(barrier, 2 * half - sub)

        @pl.when(sub == 0)
        def _():
            greet(ready, {"sub": 1})

    @pl.when(jnp.logical_and(sent[0], jnp.logical_not(last)))
    def _():
        copies[0].start()

    start(1, half, True)

    @pl.when(near)
    def _():
        right_buf[2 * slot + sub] = right

    loaded(w_v.at[:, 2 * hidden :], 3)
    left_shift = through(vec_v[1], w_v[:, 2 * hidden : 4 * hidden])
    left = gated(centred, scale, left_shift, w_v[:, 2 * hidden : 4 * hidden])
    left_buf[sub] = left.reshape(rows, cols, hidden)

    @pl.when(jnp.logical_and(high_near, jnp.logical_not(mid)))
    def _():
        pl.semaphore_wait(ready, 1)

    left_copy.start()

    @pl.when(jnp.logical_and(high_near, mid))
    def _():
        pl.semaphore_wait(barrier, half - 1)
        greet(ready, {"sub": 0})

    @pl.when(jnp.logical_and(high_far, mid))
    def _():
        pl.semaphore_wait(ready, 1)

    @pl.when(jnp.logical_not(low))
    def _():
        start(half, n_row, True)

    gate = w_v[:, 4 * hidden : 4 * hidden + chan]
    gating = jnp.dot(centred, gate, preferred_element_type=jnp.float32) * scale
    gating = sigmoid(gating + through(vec_v[1], gate)).astype(jnp.bfloat16)
    w_out = w_v[:, 5 * hidden : 6 * hidden]
    out_shift = through(vec_v[3], w_out)

    @pl.when(low_far)
    def _():
        pl.semaphore_wait(barrier, half - 1)
        greet(ready, {"sub": 0})

    @pl.when(low_near)
    def _():
        pl.semaphore_wait(ready, 1)

    @pl.when(low)
    def _():
        for q in order:
            copies[q].start()
        pl.semaphore_wait(late, 1)

    @pl.when(low_far)
    def _():
        greet(late, {"sub": 0})

    @pl.when(low)
    def _():
        copies[-1].start()

    left_copy.wait_recv()

    def arrived(group, blocks):
        pltpu.make_async_remote_copy(
            src_ref=right_buf.at[0:blocks],
            dst_ref=right_buf.at[0:blocks],
            send_sem=send_sem.at[0],
            recv_sem=recv_sem.at[group],
            device_id={"sub": other},
            device_id_type=pl.DeviceIdType.MESH,
        ).wait_recv()

    def block_of(source):
        return right_buf[2 * source : 2 * source + 2].astype(jnp.float32)

    def absorb(source, block):
        for i in range(rows):
            prod = left_buf[:, i].astype(jnp.float32)[:, None] * block
            prod = prod[0] + prod[1]
            prod = jnp.sum(prod.reshape(rows, cols // 8, 8, hidden), axis=1)
            tri_v[i, source * rows : (source + 1) * rows, :] = jnp.sum(prod, axis=1)

    def project(source):
        raw = block_of(source).reshape(2 * rows * cols, chan)
        raw_centred, raw_scale = centre(raw, vec_v[0])
        far = gated(raw_centred, raw_scale, right_shift, w_v[:, 0 : 2 * hidden])
        return far.astype(jnp.float32).reshape(2, rows, cols, hidden)

    first = jnp.logical_and(low_far, row == 0)

    @pl.when(first)
    def _():
        arrived(0, 2 * split)
        for source in range(split):
            absorb(source, block_of(source))
        arrived(1, 2 * split)
        absorb(half - 1, project(half - 1))
        for source in range(split, half - 1):
            absorb(source, block_of(source))

    @pl.when(jnp.logical_not(first))
    def _():
        for group in range(2):
            own = jnp.logical_and(near, slot // split == group)

            @pl.when(own)
            def _():
                arrived(group, 2 * split - 1)

            @pl.when(jnp.logical_not(own))
            def _():
                arrived(group, 2 * split)

            for source in range(group * split, (group + 1) * split):
                absorb(source, block_of(source))

    tri = tri_v[...].reshape(rows * cols, hidden).astype(jnp.bfloat16).astype(jnp.float32)
    tri_centred, tri_scale = centre(tri, vec_v[2])
    mixed = jnp.dot(tri_centred, w_out, preferred_element_type=jnp.float32)
    mixed = mixed * tri_scale + out_shift
    out = (gating.astype(jnp.float32) * mixed).astype(jnp.bfloat16)
    out_ref[...] = out.reshape(rows, cols, chan)

    left_copy.wait_send()
    def gone(blocks):
        pltpu.make_async_remote_copy(
            src_ref=right_buf.at[0:blocks],
            dst_ref=right_buf.at[0:blocks],
            send_sem=send_sem.at[0],
            recv_sem=recv_sem.at[0],
            device_id={"sub": other},
            device_id_type=pl.DeviceIdType.MESH,
        ).wait_send()

    @pl.when(near)
    def _():
        gone(n_row - 1)

    @pl.when(jnp.logical_not(near))
    def _():
        gone(n_row)


def one_round(n_row, pair_rep, norm_gain, norm_bias, *rest):
    w_a_proj, w_a_gate, w_b_proj, w_b_gate, w_gate, out_gain, out_bias, w_out = rest
    rows, cols, chan = pair_rep.shape
    hidden = w_a_proj.shape[1]
    half = n_row // 2
    hbm = pl.BlockSpec(memory_space=pltpu.HBM)
    return pl.pallas_call(
        functools.partial(kernel, n_row),
        out_shape=pltpu.VMEM((rows, cols, chan), jnp.bfloat16),
        in_specs=[hbm] * 11,
        out_specs=pl.BlockSpec(memory_space=pltpu.VMEM),
        scratch_shapes=[
            pltpu.VMEM((rows, cols, chan), jnp.bfloat16),
            pltpu.VMEM((4, 1, chan), jnp.float32),
            pltpu.VMEM((chan, 6 * hidden), jnp.bfloat16),
            pltpu.VMEM((rows, cols, hidden), jnp.bfloat16),
            pltpu.VMEM((2 * half, rows, cols, hidden), jnp.bfloat16),
            pltpu.VMEM((2, rows, cols, hidden), jnp.bfloat16),
            pltpu.VMEM((rows, cols, hidden), jnp.float32),
            pltpu.SemaphoreType.DMA((4,)),
            pltpu.SemaphoreType.DMA((2,)),
            pltpu.SemaphoreType.DMA((2,)),
            pltpu.SemaphoreType.DMA,
            pltpu.SemaphoreType.REGULAR,
            pltpu.SemaphoreType.REGULAR,
        ],
        compiler_params=pltpu.CompilerParams(
            collective_id=0, has_side_effects=True, vmem_limit_bytes=16 * 2**20
        ),
    )(
        *(
            pltpu.with_memory_space_constraint(operand, pltpu.HBM)
            for operand in (
                pair_rep,
                norm_gain.reshape(1, chan),
                norm_bias.reshape(1, chan),
                w_a_proj,
                w_a_gate,
                w_b_proj,
                w_b_gate,
                w_gate,
                out_gain.reshape(1, hidden),
                out_bias.reshape(1, hidden),
                w_out,
            )
        )
    )


def body(n_row, n_sub, *operands):
    rows, cols, chan = operands[0].shape
    hidden = operands[3].shape[1]
    gathered = cols * cols * n_sub * hidden * 2
    if n_sub == 2 and n_row % 4 == 0 and cols % 16 == 0 and hidden == chan and gathered <= 4 * 2**20:
        return one_round(n_row, *operands)
    return per_device(*operands)


def solution(mesh):
    in_specs = (P(("grp", "row"), "sub", None), P(), P(), P(), P(), P(), P(), P(), P(), P(), P())
    out_specs = P(("grp", "row"), "sub", None)
    return jax.shard_map(
        functools.partial(body, mesh.shape["row"], mesh.shape["sub"]),
        mesh=mesh,
        in_specs=in_specs,
        out_specs=out_specs,
        check_vma=False,
    )
```

```python
import functools

import jax
import jax.numpy as jnp
from jax import lax
from jax.experimental import pallas as pl
from jax.experimental.pallas import tpu as pltpu
from jax.sharding import PartitionSpec as P

EPSILON = 1e-05


def layer_norm(values, gain, shift, axis):
    centred = values - jnp.mean(values, axis=axis, keepdims=True)
    variance = jnp.mean(centred * centred, axis=axis, keepdims=True)
    return centred * lax.rsqrt(variance + EPSILON) * gain + shift


def per_device(
    pair_rep,
    norm_gain,
    norm_bias,
    w_a_proj,
    w_a_gate,
    w_b_proj,
    w_b_gate,
    w_gate,
    out_gain,
    out_bias,
    w_out,
):
    hidden = w_a_proj.shape[1]
    w_inner = jnp.concatenate([w_a_proj, w_a_gate, w_b_proj, w_b_gate], axis=1)
    normed = layer_norm(pair_rep.astype(jnp.float32), norm_gain, norm_bias, -1).astype(jnp.bfloat16)
    inner = jnp.einsum("rkc,cm->mrk", normed, w_inner, preferred_element_type=jnp.float32)
    left_local = (jax.nn.sigmoid(inner[hidden : 2 * hidden]) * inner[:hidden]).astype(jnp.bfloat16)
    right_local = (
        jax.nn.sigmoid(inner[3 * hidden : 4 * hidden]) * inner[2 * hidden : 3 * hidden]
    ).astype(jnp.bfloat16)
    gating = jax.nn.sigmoid(
        jnp.einsum("rkc,cd->rkd", normed, w_gate, preferred_element_type=jnp.float32)
    ).astype(jnp.bfloat16)
    left_chan, right_chan = (
        lax.all_to_all(left_local, "row", split_axis=0, concat_axis=1, tiled=True),
        lax.all_to_all(right_local, "row", split_axis=0, concat_axis=1, tiled=True),
    )
    left_rows = lax.all_to_all(left_chan, "sub", split_axis=1, concat_axis=2, tiled=True)
    triangle = jnp.einsum(
        "hik,hjk->hij",
        left_rows,
        lax.all_gather(right_chan, "sub", axis=2, tiled=True),
        preferred_element_type=jnp.float32,
    ).astype(jnp.bfloat16)
    regrouped = lax.all_to_all(
        lax.all_to_all(triangle, "sub", split_axis=2, concat_axis=1, tiled=True),
        "row",
        split_axis=1,
        concat_axis=0,
        tiled=True,
    )
    hidden_normed = layer_norm(
        regrouped.astype(jnp.float32), out_gain[:, None, None], out_bias[:, None, None], 0
    ).astype(jnp.bfloat16)
    mixed = jnp.einsum("hrj,hc->rjc", hidden_normed, w_out, preferred_element_type=jnp.float32)
    return (gating.astype(jnp.float32) * mixed).astype(jnp.bfloat16)


def sigmoid(values):
    return 0.5 * jnp.tanh(0.5 * values) + 0.5


def centre(values, gain):
    centred = values - jnp.mean(values, axis=-1, keepdims=True)
    scale = lax.rsqrt(jnp.mean(centred * centred, axis=-1, keepdims=True) + EPSILON)
    return (centred * gain).astype(jnp.bfloat16), scale


def through(shift, weights):
    high = shift.astype(jnp.bfloat16)
    low = (shift - high.astype(jnp.float32)).astype(jnp.bfloat16)
    pair = jnp.concatenate([jnp.broadcast_to(high, (8, high.shape[1])), jnp.broadcast_to(low, (8, low.shape[1]))], axis=0)
    mixed = jnp.dot(pair, weights, preferred_element_type=jnp.float32)
    return mixed[0:1] + mixed[8:9]


def gated(centred, scale, shift, weights):
    hidden = weights.shape[1] // 2
    inner = jnp.dot(centred, weights, preferred_element_type=jnp.float32) * scale + shift
    return (sigmoid(inner[:, hidden:]) * inner[:, :hidden]).astype(jnp.bfloat16)


def kernel(
    n_row,
    pair_hbm,
    ngain_hbm,
    nbias_hbm,
    wap_hbm,
    wag_hbm,
    wbp_hbm,
    wbg_hbm,
    wg_hbm,
    ogain_hbm,
    obias_hbm,
    wo_hbm,
    out_ref,
    pair_v,
    vec_v,
    w_v,
    right_send,
    right_buf,
    left_buf,
    tri_v,
    in_sem,
    send_sem,
    recv_sem,
    ready,
    late,
    bytes_v,
    fold_v,
):
    rows, cols, chan = pair_v.shape
    hidden = right_send.shape[-1]
    half = n_row // 2
    row = lax.axis_index("row")
    sub = lax.axis_index("sub")
    other = 1 - sub
    owner = row // half
    slot = lax.rem(row, half)
    near = sub == owner
    low = owner == 0
    low_near = jnp.logical_and(low, sub == 0)
    low_far = jnp.logical_and(low, sub == 1)
    high_near = jnp.logical_and(owner == 1, sub == 1)
    high_far = jnp.logical_and(owner == 1, sub == 0)
    last = row == n_row - 1
    first = jnp.logical_and(low_far, row == 0)
    split = half // 2
    order = [half + q for pair in zip(range(split), range(split, half - 1)) for q in pair]
    order += [q for q in range(half, n_row - 1) if q not in order]
    mid = jnp.logical_and(owner == 1, slot < split)
    outer = jnp.logical_and(owner == 1, jnp.logical_and(slot >= split, jnp.logical_not(last)))

    weights = (wbp_hbm, wbg_hbm, wap_hbm, wag_hbm, wg_hbm, wo_hbm)
    loads = [pltpu.make_async_copy(pair_hbm, pair_v, in_sem.at[0])]
    for n, vector in enumerate((ngain_hbm, nbias_hbm, ogain_hbm, obias_hbm)):
        loads.append(pltpu.make_async_copy(vector, vec_v.at[n], in_sem.at[0]))
    for n, weight in enumerate(weights):
        span = w_v.at[:, n * hidden : (n + 1) * hidden]
        loads.append(pltpu.make_async_copy(weight, span, in_sem.at[1 if n < 2 else 2]))

    def loaded(span, index):
        pltpu.make_async_copy(span, span, in_sem.at[index]).wait()

    barrier = pltpu.get_barrier_semaphore()

    def greet(semaphore, target):
        pl.semaphore_signal(
            semaphore, inc=1, device_id=target, device_id_type=pl.DeviceIdType.MESH
        )

    left_copy = pltpu.make_async_remote_copy(
        src_ref=left_buf.at[sub],
        dst_ref=left_buf.at[sub],
        send_sem=in_sem.at[0],
        recv_sem=recv_sem.at[0],
        device_id={"sub": other},
        device_id_type=pl.DeviceIdType.MESH,
    )

    def block_copy(source, target_row, target_sub):
        return pltpu.make_async_remote_copy(
            src_ref=source,
            dst_ref=right_buf.at[2 * slot + sub],
            send_sem=send_sem,
            recv_sem=recv_sem.at[slot // split],
            device_id={"row": target_row, "sub": target_sub},
            device_id_type=pl.DeviceIdType.MESH,
        )

    raw_copy = block_copy(pair_hbm, 0, owner)
    copies = [block_copy(right_send, q, owner) for q in range(n_row)]
    sent = [jnp.logical_not(jnp.logical_and(near, row == q)) for q in range(n_row)]

    def start(first, end, guarded):
        for q in range(first, end):
            if guarded:

                @pl.when(sent[q])
                def _():
                    copies[q].start()
            else:
                copies[q].start()

    @pl.when(low_far)
    def _():
        greet(barrier, {"sub": 0})
        for step in range(half)[::-1]:
            greet(barrier, {"row": half + step, "sub": 0})
            if step >= split:
                greet(barrier, {"row": half + step, "sub": 1})

    @pl.when(high_near)
    def _():
        greet(barrier, {"sub": 0})
        for step in range(half):

            @pl.when(slot != step)
            def _():
                greet(barrier, {"row": half + step, "sub": 1})
                if step >= split:
                    greet(barrier, {"row": half + step, "sub": 0})

    @pl.when(last)
    def _():
        pl.semaphore_wait(barrier, 2 * half - sub)
        raw_copy.start()

        @pl.when(sub == 0)
        def _():
            greet(ready, {"sub": 1})
            for step in range(half):
                greet(late, {"row": step, "sub": 1})

    @pl.when(jnp.logical_and(high_far, jnp.logical_not(last)))
    def _():
        for step in range(half):
            greet(barrier, {"row": step, "sub": 1})

    @pl.when(low_near)
    def _():
        for step in range(1, half):
            greet(barrier, {"row": lax.rem(slot + step, half), "sub": 0})

    for load in loads:
        load.start()

    @pl.when(low_near)
    def _():
        pl.semaphore_wait(barrier, half)
        greet(ready, {"sub": 1})

    @pl.when(jnp.logical_and(high_far, mid))
    def _():
        pl.semaphore_wait(barrier, half + 1)
        greet(ready, {"sub": 1})

    loaded(bytes_v, 0)
    pair = pair_v[...].astype(jnp.float32).reshape(rows * cols, chan)
    centred, scale = centre(pair, vec_v[0])
    loaded(w_v.at[:, 0 : 2 * hidden], 1)
    right_shift = through(vec_v[1], w_v[:, 0 : 2 * hidden])
    right = gated(centred, scale, right_shift, w_v[:, 0 : 2 * hidden])
    right = right.reshape(rows, cols, hidden)
    right_send[...] = right

    @pl.when(low_far)
    def _():
        pl.semaphore_wait(ready, 1)

    @pl.when(jnp.logical_and(high_near, mid))
    def _():
        pl.semaphore_wait(ready, 1)

    @pl.when(outer)
    def _():
        pl.semaphore_wait(barrier, 2 * half - sub)

        @pl.when(sub == 0)
        def _():
            greet(ready, {"sub": 1})

    @pl.when(jnp.logical_and(sent[0], jnp.logical_not(last)))
    def _():
        copies[0].start()

    start(1, half, True)

    @pl.when(near)
    def _():
        right_buf[2 * slot + sub] = right

    loaded(w_v.at[:, 2 * hidden :], 2)
    left_shift = through(vec_v[1], w_v[:, 2 * hidden : 4 * hidden])
    left = gated(centred, scale, left_shift, w_v[:, 2 * hidden : 4 * hidden])
    left_buf[sub] = left.reshape(rows, cols, hidden)

    @pl.when(jnp.logical_and(high_near, jnp.logical_not(mid)))
    def _():
        pl.semaphore_wait(ready, 1)

    left_copy.start()

    @pl.when(jnp.logical_and(high_near, mid))
    def _():
        pl.semaphore_wait(barrier, half - 1)
        greet(ready, {"sub": 0})

    @pl.when(jnp.logical_and(high_far, mid))
    def _():
        pl.semaphore_wait(ready, 1)

    @pl.when(jnp.logical_not(low))
    def _():
        start(half, n_row, True)

    gate = w_v[:, 4 * hidden : 4 * hidden + chan]
    gating = jnp.dot(centred, gate, preferred_element_type=jnp.float32) * scale
    gating = sigmoid(gating + through(vec_v[1], gate)).astype(jnp.bfloat16)
    @pl.when(first)
    def _():
        gain = jnp.broadcast_to(vec_v[0], (chan, chan)).T[:, 0:1]
        folded = w_v[:, 0 : 2 * hidden].astype(jnp.float32) * gain
        folded = folded - jnp.mean(folded, axis=0, keepdims=True)
        high = folded.astype(jnp.bfloat16)
        fold_v[0:chan] = high
        fold_v[chan:] = (folded - high.astype(jnp.float32)).astype(jnp.bfloat16)

    w_out = w_v[:, 5 * hidden : 6 * hidden]
    out_shift = through(vec_v[3], w_out)

    @pl.when(low_far)
    def _():
        pl.semaphore_wait(barrier, half - 1)
        greet(ready, {"sub": 0})

    @pl.when(low_near)
    def _():
        pl.semaphore_wait(ready, 1)

    @pl.when(low)
    def _():
        for q in order:
            copies[q].start()
        pl.semaphore_wait(late, 1)

    @pl.when(low_far)
    def _():
        greet(late, {"sub": 0})

    @pl.when(low)
    def _():
        copies[-1].start()


    def arrived(group, blocks):
        pltpu.make_async_remote_copy(
            src_ref=right_buf.at[0:blocks],
            dst_ref=right_buf.at[0:blocks],
            send_sem=send_sem,
            recv_sem=recv_sem.at[group],
            device_id={"sub": other},
            device_id_type=pl.DeviceIdType.MESH,
        ).wait_recv()

    def block_of(source):
        return right_buf[2 * source : 2 * source + 2].astype(jnp.float32)

    def absorb(source, block):
        for i in range(rows):
            prod = left_buf[:, i].astype(jnp.float32)[:, None] * block
            prod = prod[0] + prod[1]
            prod = jnp.sum(prod.reshape(rows, cols // 8, 8, hidden), axis=1)
            tri_v[i, source * rows : (source + 1) * rows, :] = jnp.sum(prod, axis=1)

    def project(source):
        bits = right_buf[2 * source : 2 * source + 2].reshape(2 * rows * cols, chan)
        raw = bits.astype(jnp.float32)
        moved = raw - jnp.mean(raw, axis=-1, keepdims=True)
        raw_scale = lax.rsqrt(jnp.mean(moved * moved, axis=-1, keepdims=True) + EPSILON)
        twice = jnp.concatenate([bits, bits], axis=1)
        far = gated(twice, raw_scale, right_shift, fold_v[...])
        return far.astype(jnp.float32).reshape(2, rows, cols, hidden)


    @pl.when(first)
    def _():
        arrived(0, 2 * split + 1)
        for source in range(split):
            absorb(source, block_of(source))
        arrived(1, 2 * split)
        absorb(half - 1, project(half - 1))
        for source in range(split, half - 1):
            absorb(source, block_of(source))

    @pl.when(jnp.logical_not(first))
    def _():
        for group in range(2):
            own = jnp.logical_and(near, slot // split == group)

            @pl.when(own)
            def _():
                arrived(group, 2 * split - group)

            @pl.when(jnp.logical_not(own))
            def _():
                arrived(group, 2 * split + 1 - group)

            for source in range(group * split, (group + 1) * split):
                absorb(source, block_of(source))

    tri = tri_v[...].reshape(rows * cols, hidden).astype(jnp.bfloat16).astype(jnp.float32)
    tri_centred, tri_scale = centre(tri, vec_v[2])
    mixed = jnp.dot(tri_centred, w_out, preferred_element_type=jnp.float32)
    mixed = mixed * tri_scale + out_shift
    out = (gating.astype(jnp.float32) * mixed).astype(jnp.bfloat16)
    out_ref[...] = out.reshape(rows, cols, chan)

    left_copy.wait_send()
    def gone(blocks):
        pltpu.make_async_remote_copy(
            src_ref=right_buf.at[0:blocks],
            dst_ref=right_buf.at[0:blocks],
            send_sem=send_sem,
            recv_sem=recv_sem.at[0],
            device_id={"sub": other},
            device_id_type=pl.DeviceIdType.MESH,
        ).wait_send()

    @pl.when(near)
    def _():
        gone(n_row - 1)

    @pl.when(jnp.logical_not(near))
    def _():
        gone(n_row)


def one_round(n_row, pair_rep, norm_gain, norm_bias, *rest):
    w_a_proj, w_a_gate, w_b_proj, w_b_gate, w_gate, out_gain, out_bias, w_out = rest
    rows, cols, chan = pair_rep.shape
    hidden = w_a_proj.shape[1]
    half = n_row // 2
    hbm = pl.BlockSpec(memory_space=pltpu.HBM)
    return pl.pallas_call(
        functools.partial(kernel, n_row),
        out_shape=pltpu.VMEM((rows, cols, chan), jnp.bfloat16),
        in_specs=[hbm] * 11,
        out_specs=pl.BlockSpec(memory_space=pltpu.VMEM),
        scratch_shapes=[
            pltpu.VMEM((rows, cols, chan), jnp.bfloat16),
            pltpu.VMEM((4, 1, chan), jnp.float32),
            pltpu.VMEM((chan, 6 * hidden), jnp.bfloat16),
            pltpu.VMEM((rows, cols, hidden), jnp.bfloat16),
            pltpu.VMEM((2 * half, rows, cols, hidden), jnp.bfloat16),
            pltpu.VMEM((2, rows, cols, hidden), jnp.bfloat16),
            pltpu.VMEM((rows, cols, hidden), jnp.float32),
            pltpu.SemaphoreType.DMA((3,)),
            pltpu.SemaphoreType.DMA,
            pltpu.SemaphoreType.DMA((2,)),
            pltpu.SemaphoreType.REGULAR,
            pltpu.SemaphoreType.REGULAR,
            pltpu.VMEM((rows * cols + 8, chan), jnp.bfloat16),
            pltpu.VMEM((2 * chan, 2 * hidden), jnp.bfloat16),
        ],
        compiler_params=pltpu.CompilerParams(
            collective_id=0, has_side_effects=True, vmem_limit_bytes=16 * 2**20
        ),
    )(
        *(
            pltpu.with_memory_space_constraint(operand, pltpu.HBM)
            for operand in (
                pair_rep,
                norm_gain.reshape(1, chan),
                norm_bias.reshape(1, chan),
                w_a_proj,
                w_a_gate,
                w_b_proj,
                w_b_gate,
                w_gate,
                out_gain.reshape(1, hidden),
                out_bias.reshape(1, hidden),
                w_out,
            )
        )
    )


def body(n_row, n_sub, *operands):
    rows, cols, chan = operands[0].shape
    hidden = operands[3].shape[1]
    gathered = cols * cols * n_sub * hidden * 2
    if n_sub == 2 and n_row % 4 == 0 and cols % 16 == 0 and hidden == chan and gathered <= 4 * 2**20:
        return one_round(n_row, *operands)
    return per_device(*operands)


def solution(mesh):
    in_specs = (P(("grp", "row"), "sub", None), P(), P(), P(), P(), P(), P(), P(), P(), P(), P())
    out_specs = P(("grp", "row"), "sub", None)
    return jax.shard_map(
        functools.partial(body, mesh.shape["row"], mesh.shape["sub"]),
        mesh=mesh,
        in_specs=in_specs,
        out_specs=out_specs,
        check_vma=False,
    )
```

```python
import functools

import jax
import jax.numpy as jnp
from jax import lax
from jax.experimental import pallas as pl
from jax.experimental.pallas import tpu as pltpu
from jax.sharding import PartitionSpec as P

EPSILON = 1e-05


def layer_norm(values, gain, shift, axis):
    centred = values - jnp.mean(values, axis=axis, keepdims=True)
    variance = jnp.mean(centred * centred, axis=axis, keepdims=True)
    return centred * lax.rsqrt(variance + EPSILON) * gain + shift


def per_device(
    pair_rep,
    norm_gain,
    norm_bias,
    w_a_proj,
    w_a_gate,
    w_b_proj,
    w_b_gate,
    w_gate,
    out_gain,
    out_bias,
    w_out,
):
    hidden = w_a_proj.shape[1]
    w_inner = jnp.concatenate([w_a_proj, w_a_gate, w_b_proj, w_b_gate], axis=1)
    normed = layer_norm(pair_rep.astype(jnp.float32), norm_gain, norm_bias, -1).astype(jnp.bfloat16)
    inner = jnp.einsum("rkc,cm->mrk", normed, w_inner, preferred_element_type=jnp.float32)
    left_local = (jax.nn.sigmoid(inner[hidden : 2 * hidden]) * inner[:hidden]).astype(jnp.bfloat16)
    right_local = (
        jax.nn.sigmoid(inner[3 * hidden : 4 * hidden]) * inner[2 * hidden : 3 * hidden]
    ).astype(jnp.bfloat16)
    gating = jax.nn.sigmoid(
        jnp.einsum("rkc,cd->rkd", normed, w_gate, preferred_element_type=jnp.float32)
    ).astype(jnp.bfloat16)
    left_chan, right_chan = (
        lax.all_to_all(left_local, "row", split_axis=0, concat_axis=1, tiled=True),
        lax.all_to_all(right_local, "row", split_axis=0, concat_axis=1, tiled=True),
    )
    left_rows = lax.all_to_all(left_chan, "sub", split_axis=1, concat_axis=2, tiled=True)
    triangle = jnp.einsum(
        "hik,hjk->hij",
        left_rows,
        lax.all_gather(right_chan, "sub", axis=2, tiled=True),
        preferred_element_type=jnp.float32,
    ).astype(jnp.bfloat16)
    regrouped = lax.all_to_all(
        lax.all_to_all(triangle, "sub", split_axis=2, concat_axis=1, tiled=True),
        "row",
        split_axis=1,
        concat_axis=0,
        tiled=True,
    )
    hidden_normed = layer_norm(
        regrouped.astype(jnp.float32), out_gain[:, None, None], out_bias[:, None, None], 0
    ).astype(jnp.bfloat16)
    mixed = jnp.einsum("hrj,hc->rjc", hidden_normed, w_out, preferred_element_type=jnp.float32)
    return (gating.astype(jnp.float32) * mixed).astype(jnp.bfloat16)


def sigmoid(values):
    return 0.5 * jnp.tanh(0.5 * values) + 0.5


def centre(values, gain):
    centred = values - jnp.mean(values, axis=-1, keepdims=True)
    scale = lax.rsqrt(jnp.mean(centred * centred, axis=-1, keepdims=True) + EPSILON)
    return (centred * gain).astype(jnp.bfloat16), scale


def through(shift, weights):
    high = shift.astype(jnp.bfloat16)
    low = (shift - high.astype(jnp.float32)).astype(jnp.bfloat16)
    pair = jnp.concatenate([jnp.broadcast_to(high, (8, high.shape[1])), jnp.broadcast_to(low, (8, low.shape[1]))], axis=0)
    mixed = jnp.dot(pair, weights, preferred_element_type=jnp.float32)
    return mixed[0:1] + mixed[8:9]


def gated(centred, scale, shift, weights):
    hidden = weights.shape[1] // 2
    inner = jnp.dot(centred, weights, preferred_element_type=jnp.float32) * scale + shift
    return (sigmoid(inner[:, hidden:]) * inner[:, :hidden]).astype(jnp.bfloat16)


def kernel(
    n_row,
    pair_hbm,
    ngain_hbm,
    nbias_hbm,
    wap_hbm,
    wag_hbm,
    wbp_hbm,
    wbg_hbm,
    wg_hbm,
    ogain_hbm,
    obias_hbm,
    wo_hbm,
    out_ref,
    pair_v,
    vec_v,
    w_v,
    right_send,
    right_buf,
    left_buf,
    tri_v,
    in_sem,
    send_sem,
    recv_sem,
    ready,
    late,
    bytes_v,
    fold_v,
):
    rows, cols, chan = pair_v.shape
    hidden = right_send.shape[-1]
    half = n_row // 2
    row = lax.axis_index("row")
    sub = lax.axis_index("sub")
    other = 1 - sub
    owner = row // half
    slot = lax.rem(row, half)
    near = sub == owner
    low = owner == 0
    low_near = jnp.logical_and(low, sub == 0)
    low_far = jnp.logical_and(low, sub == 1)
    high_near = jnp.logical_and(owner == 1, sub == 1)
    high_far = jnp.logical_and(owner == 1, sub == 0)
    last = row == n_row - 1
    first = jnp.logical_and(low_far, row == 0)
    split = half // 2
    order = [half + q for pair in zip(range(split), range(split, half - 1)) for q in pair]
    order += [q for q in range(half, n_row - 1) if q not in order]
    mid = jnp.logical_and(owner == 1, slot < split)
    outer = jnp.logical_and(owner == 1, jnp.logical_and(slot >= split, jnp.logical_not(last)))

    weights = (wbp_hbm, wbg_hbm, wap_hbm, wag_hbm, wg_hbm, wo_hbm)
    loads = [pltpu.make_async_copy(pair_hbm, pair_v, in_sem.at[0])]
    for n, vector in enumerate((ngain_hbm, nbias_hbm, ogain_hbm, obias_hbm)):
        loads.append(pltpu.make_async_copy(vector, vec_v.at[n], in_sem.at[0]))
    for n, weight in enumerate(weights):
        span = w_v.at[:, n * hidden : (n + 1) * hidden]
        loads.append(pltpu.make_async_copy(weight, span, in_sem.at[1 if n < 2 else 2]))

    def loaded(span, index):
        pltpu.make_async_copy(span, span, in_sem.at[index]).wait()

    barrier = pltpu.get_barrier_semaphore()

    def greet(semaphore, target):
        pl.semaphore_signal(
            semaphore, inc=1, device_id=target, device_id_type=pl.DeviceIdType.MESH
        )

    left_copy = pltpu.make_async_remote_copy(
        src_ref=left_buf.at[sub],
        dst_ref=left_buf.at[sub],
        send_sem=in_sem.at[0],
        recv_sem=recv_sem.at[0],
        device_id={"sub": other},
        device_id_type=pl.DeviceIdType.MESH,
    )

    def block_copy(source, target_row, target_sub):
        return pltpu.make_async_remote_copy(
            src_ref=source,
            dst_ref=right_buf.at[2 * slot + sub],
            send_sem=send_sem,
            recv_sem=recv_sem.at[slot // split],
            device_id={"row": target_row, "sub": target_sub},
            device_id_type=pl.DeviceIdType.MESH,
        )

    raw_copy = block_copy(pair_hbm, 0, owner)
    copies = [block_copy(right_send, q, owner) for q in range(n_row)]
    sent = [jnp.logical_not(jnp.logical_and(near, row == q)) for q in range(n_row)]

    def start(first, end, guarded):
        for q in range(first, end):
            if guarded:

                @pl.when(sent[q])
                def _():
                    copies[q].start()
            else:
                copies[q].start()

    @pl.when(low_far)
    def _():
        greet(barrier, {"sub": 0})
        for step in range(half)[::-1]:
            greet(barrier, {"row": half + step, "sub": 0})
            if step >= split:
                greet(barrier, {"row": half + step, "sub": 1})

    @pl.when(high_near)
    def _():
        greet(barrier, {"sub": 0})
        for step in range(half):

            @pl.when(slot != step)
            def _():
                greet(barrier, {"row": half + step, "sub": 1})
                if step >= split:
                    greet(barrier, {"row": half + step, "sub": 0})

    @pl.when(last)
    def _():
        pl.semaphore_wait(barrier, 2 * half - sub)
        raw_copy.start()

        @pl.when(sub == 0)
        def _():
            greet(ready, {"sub": 1})
            for step in range(half):
                greet(late, {"row": step, "sub": 1})

    @pl.when(jnp.logical_and(high_far, jnp.logical_not(last)))
    def _():
        for step in range(half):
            greet(barrier, {"row": step, "sub": 1})

    @pl.when(low_near)
    def _():
        for step in range(1, half):
            greet(barrier, {"row": lax.rem(slot + step, half), "sub": 0})

    for load in loads:
        load.start()

    @pl.when(low_near)
    def _():
        pl.semaphore_wait(barrier, half)
        greet(ready, {"sub": 1})

    @pl.when(jnp.logical_and(high_far, mid))
    def _():
        pl.semaphore_wait(barrier, half + 1)
        greet(ready, {"sub": 1})

    loaded(bytes_v, 0)
    pair = pair_v[...].astype(jnp.float32).reshape(rows * cols, chan)
    centred, scale = centre(pair, vec_v[0])
    loaded(w_v.at[:, 0 : 2 * hidden], 1)
    right_shift = through(vec_v[1], w_v[:, 0 : 2 * hidden])
    right = gated(centred, scale, right_shift, w_v[:, 0 : 2 * hidden])
    right = right.reshape(rows, cols, hidden)
    right_send[...] = right

    @pl.when(low_far)
    def _():
        pl.semaphore_wait(ready, 1)

    @pl.when(jnp.logical_and(high_near, mid))
    def _():
        pl.semaphore_wait(ready, 1)

    @pl.when(outer)
    def _():
        pl.semaphore_wait(barrier, 2 * half - sub)

        @pl.when(sub == 0)
        def _():
            greet(ready, {"sub": 1})

    @pl.when(jnp.logical_and(sent[0], jnp.logical_not(last)))
    def _():
        copies[0].start()

    start(1, half, True)

    @pl.when(near)
    def _():
        right_buf[2 * slot + sub] = right

    loaded(w_v.at[:, 2 * hidden :], 2)
    left_shift = through(vec_v[1], w_v[:, 2 * hidden : 4 * hidden])
    left = gated(centred, scale, left_shift, w_v[:, 2 * hidden : 4 * hidden])
    left_buf[sub] = left.reshape(rows, cols, hidden)

    @pl.when(jnp.logical_and(high_near, jnp.logical_not(mid)))
    def _():
        pl.semaphore_wait(ready, 1)

    left_copy.start()

    @pl.when(jnp.logical_and(high_near, mid))
    def _():
        pl.semaphore_wait(barrier, half - 1)
        greet(ready, {"sub": 0})

    @pl.when(jnp.logical_and(high_far, mid))
    def _():
        pl.semaphore_wait(ready, 1)

    @pl.when(jnp.logical_not(low))
    def _():
        start(half, n_row, True)

    gate = w_v[:, 4 * hidden : 4 * hidden + chan]
    gating = jnp.dot(centred, gate, preferred_element_type=jnp.float32) * scale
    gating = sigmoid(gating + through(vec_v[1], gate)).astype(jnp.bfloat16)
    @pl.when(first)
    def _():
        gain = jnp.broadcast_to(vec_v[0], (chan, chan)).T[:, 0:1]
        folded = w_v[:, 0 : 2 * hidden].astype(jnp.float32) * gain
        folded = folded - jnp.mean(folded, axis=0, keepdims=True)
        high = folded.astype(jnp.bfloat16)
        fold_v[0:chan] = high
        fold_v[chan:] = (folded - high.astype(jnp.float32)).astype(jnp.bfloat16)

    w_out = w_v[:, 5 * hidden : 6 * hidden]
    out_shift = through(vec_v[3], w_out)

    @pl.when(low_far)
    def _():
        pl.semaphore_wait(barrier, half - 1)
        greet(ready, {"sub": 0})

    @pl.when(low_near)
    def _():
        pl.semaphore_wait(ready, 1)

    @pl.when(low)
    def _():
        for q in order:
            copies[q].start()
        pl.semaphore_wait(late, 1)

    @pl.when(low_far)
    def _():
        greet(late, {"sub": 0})

    @pl.when(low)
    def _():
        copies[-1].start()


    def arrived(group, blocks):
        pltpu.make_async_remote_copy(
            src_ref=right_buf.at[0:blocks],
            dst_ref=right_buf.at[0:blocks],
            send_sem=send_sem,
            recv_sem=recv_sem.at[group],
            device_id={"sub": other},
            device_id_type=pl.DeviceIdType.MESH,
        ).wait_recv()

    def block_of(source):
        return right_buf[2 * source : 2 * source + 2].astype(jnp.float32)

    def absorb(source, block):
        for i in range(rows):
            prod = left_buf[:, i].astype(jnp.float32)[:, None] * block
            prod = prod[0] + prod[1]
            prod = jnp.sum(prod.reshape(rows, cols // 8, 8, hidden), axis=1)
            tri_v[i, source * rows : (source + 1) * rows, :] = jnp.sum(prod, axis=1)

    def project(source):
        bits = right_buf[2 * source : 2 * source + 2].reshape(2 * rows * cols, chan)
        raw = bits.astype(jnp.float32)
        moved = raw - jnp.mean(raw, axis=-1, keepdims=True)
        raw_scale = lax.rsqrt(jnp.mean(moved * moved, axis=-1, keepdims=True) + EPSILON)
        twice = jnp.concatenate([bits, bits], axis=1)
        far = gated(twice, raw_scale, right_shift, fold_v[...])
        return far.astype(jnp.float32).reshape(2, rows, cols, hidden)


    @pl.when(first)
    def _():
        arrived(0, 2 * split + 1)
        for source in range(split):
            absorb(source, block_of(source))
        arrived(1, 2 * split)
        absorb(half - 1, project(half - 1))
        for source in range(split, half - 1):
            absorb(source, block_of(source))

    @pl.when(jnp.logical_not(first))
    def _():
        for group in range(2):
            own = jnp.logical_and(near, slot // split == group)

            @pl.when(own)
            def _():
                arrived(group, 2 * split - group)

            @pl.when(jnp.logical_not(own))
            def _():
                arrived(group, 2 * split + 1 - group)

            for source in range(group * split, (group + 1) * split):
                absorb(source, block_of(source))

    tri = tri_v[...].reshape(rows * cols, hidden).astype(jnp.bfloat16).astype(jnp.float32)
    tri_centred, tri_scale = centre(tri, vec_v[2])
    mixed = jnp.dot(tri_centred, w_out, preferred_element_type=jnp.float32)
    mixed = mixed * tri_scale + out_shift
    out = (gating.astype(jnp.float32) * mixed).astype(jnp.bfloat16)
    out_ref[...] = out.reshape(rows, cols, chan)

    left_copy.wait_send()
    def gone(blocks):
        pltpu.make_async_remote_copy(
            src_ref=right_buf.at[0:blocks],
            dst_ref=right_buf.at[0:blocks],
            send_sem=send_sem,
            recv_sem=recv_sem.at[0],
            device_id={"sub": other},
            device_id_type=pl.DeviceIdType.MESH,
        ).wait_send()

    @pl.when(near)
    def _():
        gone(n_row - 1)

    @pl.when(jnp.logical_not(near))
    def _():
        gone(n_row)


def one_round(n_row, pair_rep, norm_gain, norm_bias, *rest):
    w_a_proj, w_a_gate, w_b_proj, w_b_gate, w_gate, out_gain, out_bias, w_out = rest
    rows, cols, chan = pair_rep.shape
    hidden = w_a_proj.shape[1]
    half = n_row // 2
    hbm = pl.BlockSpec(memory_space=pltpu.HBM)
    return pl.pallas_call(
        functools.partial(kernel, n_row),
        out_shape=pltpu.VMEM((rows, cols, chan), jnp.bfloat16),
        in_specs=[hbm] * 11,
        out_specs=pl.BlockSpec(memory_space=pltpu.VMEM),
        scratch_shapes=[
            pltpu.VMEM((rows, cols, chan), jnp.bfloat16),
            pltpu.VMEM((4, 1, chan), jnp.float32),
            pltpu.VMEM((chan, 6 * hidden), jnp.bfloat16),
            pltpu.VMEM((rows, cols, hidden), jnp.bfloat16),
            pltpu.VMEM((2 * half, rows, cols, hidden), jnp.bfloat16),
            pltpu.VMEM((2, rows, cols, hidden), jnp.bfloat16),
            pltpu.VMEM((rows, cols, hidden), jnp.float32),
            pltpu.SemaphoreType.DMA((3,)),
            pltpu.SemaphoreType.DMA,
            pltpu.SemaphoreType.DMA((2,)),
            pltpu.SemaphoreType.REGULAR,
            pltpu.SemaphoreType.REGULAR,
            pltpu.VMEM((rows * cols // 2 + 4, 1, chan), jnp.float32),
            pltpu.VMEM((2 * chan, 2 * hidden), jnp.bfloat16),
        ],
        compiler_params=pltpu.CompilerParams(
            collective_id=0, has_side_effects=True, vmem_limit_bytes=16 * 2**20
        ),
    )(
        *(
            pltpu.with_memory_space_constraint(operand, pltpu.HBM)
            for operand in (
                pair_rep,
                norm_gain.reshape(1, chan),
                norm_bias.reshape(1, chan),
                w_a_proj,
                w_a_gate,
                w_b_proj,
                w_b_gate,
                w_gate,
                out_gain.reshape(1, hidden),
                out_bias.reshape(1, hidden),
                w_out,
            )
        )
    )


def body(n_row, n_sub, *operands):
    rows, cols, chan = operands[0].shape
    hidden = operands[3].shape[1]
    gathered = cols * cols * n_sub * hidden * 2
    if n_sub == 2 and n_row % 4 == 0 and cols % 16 == 0 and hidden == chan and gathered <= 4 * 2**20:
        return one_round(n_row, *operands)
    return per_device(*operands)


def solution(mesh):
    in_specs = (P(("grp", "row"), "sub", None), P(), P(), P(), P(), P(), P(), P(), P(), P(), P())
    out_specs = P(("grp", "row"), "sub", None)
    return jax.shard_map(
        functools.partial(body, mesh.shape["row"], mesh.shape["sub"]),
        mesh=mesh,
        in_specs=in_specs,
        out_specs=out_specs,
        check_vma=False,
    )
```

```python
import functools

import jax
import jax.numpy as jnp
from jax import lax
from jax.experimental import pallas as pl
from jax.experimental.pallas import tpu as pltpu
from jax.sharding import PartitionSpec as P

EPSILON = 1e-05


def layer_norm(values, gain, shift, axis):
    centred = values - jnp.mean(values, axis=axis, keepdims=True)
    variance = jnp.mean(centred * centred, axis=axis, keepdims=True)
    return centred * lax.rsqrt(variance + EPSILON) * gain + shift


def per_device(
    pair_rep,
    norm_gain,
    norm_bias,
    w_a_proj,
    w_a_gate,
    w_b_proj,
    w_b_gate,
    w_gate,
    out_gain,
    out_bias,
    w_out,
):
    hidden = w_a_proj.shape[1]
    w_inner = jnp.concatenate([w_a_proj, w_a_gate, w_b_proj, w_b_gate], axis=1)
    normed = layer_norm(pair_rep.astype(jnp.float32), norm_gain, norm_bias, -1).astype(jnp.bfloat16)
    inner = jnp.einsum("rkc,cm->mrk", normed, w_inner, preferred_element_type=jnp.float32)
    left_local = (jax.nn.sigmoid(inner[hidden : 2 * hidden]) * inner[:hidden]).astype(jnp.bfloat16)
    right_local = (
        jax.nn.sigmoid(inner[3 * hidden : 4 * hidden]) * inner[2 * hidden : 3 * hidden]
    ).astype(jnp.bfloat16)
    gating = jax.nn.sigmoid(
        jnp.einsum("rkc,cd->rkd", normed, w_gate, preferred_element_type=jnp.float32)
    ).astype(jnp.bfloat16)
    left_chan, right_chan = (
        lax.all_to_all(left_local, "row", split_axis=0, concat_axis=1, tiled=True),
        lax.all_to_all(right_local, "row", split_axis=0, concat_axis=1, tiled=True),
    )
    left_rows = lax.all_to_all(left_chan, "sub", split_axis=1, concat_axis=2, tiled=True)
    triangle = jnp.einsum(
        "hik,hjk->hij",
        left_rows,
        lax.all_gather(right_chan, "sub", axis=2, tiled=True),
        preferred_element_type=jnp.float32,
    ).astype(jnp.bfloat16)
    regrouped = lax.all_to_all(
        lax.all_to_all(triangle, "sub", split_axis=2, concat_axis=1, tiled=True),
        "row",
        split_axis=1,
        concat_axis=0,
        tiled=True,
    )
    hidden_normed = layer_norm(
        regrouped.astype(jnp.float32), out_gain[:, None, None], out_bias[:, None, None], 0
    ).astype(jnp.bfloat16)
    mixed = jnp.einsum("hrj,hc->rjc", hidden_normed, w_out, preferred_element_type=jnp.float32)
    return (gating.astype(jnp.float32) * mixed).astype(jnp.bfloat16)


def sigmoid(values):
    return 0.5 * jnp.tanh(0.5 * values) + 0.5


def centre(values, gain):
    centred = values - jnp.mean(values, axis=-1, keepdims=True)
    scale = lax.rsqrt(jnp.mean(centred * centred, axis=-1, keepdims=True) + EPSILON)
    return (centred * gain).astype(jnp.bfloat16), scale


def through(shift, weights):
    high = shift.astype(jnp.bfloat16)
    low = (shift - high.astype(jnp.float32)).astype(jnp.bfloat16)
    pair = jnp.concatenate([jnp.broadcast_to(high, (8, high.shape[1])), jnp.broadcast_to(low, (8, low.shape[1]))], axis=0)
    mixed = jnp.dot(pair, weights, preferred_element_type=jnp.float32)
    return mixed[0:1] + mixed[8:9]


def gated(centred, scale, shift, weights):
    hidden = weights.shape[1] // 2
    inner = jnp.dot(centred, weights, preferred_element_type=jnp.float32) * scale + shift
    return (sigmoid(inner[:, hidden:]) * inner[:, :hidden]).astype(jnp.bfloat16)


def kernel(
    n_row,
    pair_hbm,
    ngain_hbm,
    nbias_hbm,
    wap_hbm,
    wag_hbm,
    wbp_hbm,
    wbg_hbm,
    wg_hbm,
    ogain_hbm,
    obias_hbm,
    wo_hbm,
    out_ref,
    pair_v,
    vec_v,
    w_v,
    right_send,
    right_buf,
    left_buf,
    tri_v,
    in_sem,
    send_sem,
    recv_sem,
    ready,
    late,
    bytes_v,
    fold_v,
):
    rows, cols, chan = pair_v.shape
    hidden = right_send.shape[-1]
    half = n_row // 2
    row = lax.axis_index("row")
    sub = lax.axis_index("sub")
    other = 1 - sub
    owner = row // half
    slot = lax.rem(row, half)
    near = sub == owner
    low = owner == 0
    low_near = jnp.logical_and(low, sub == 0)
    low_far = jnp.logical_and(low, sub == 1)
    high_near = jnp.logical_and(owner == 1, sub == 1)
    high_far = jnp.logical_and(owner == 1, sub == 0)
    last = row == n_row - 1
    first = jnp.logical_and(low_far, row == 0)
    split = half // 2
    order = [half + q for pair in zip(range(split), range(split, half - 1)) for q in pair]
    order += [q for q in range(half, n_row - 1) if q not in order]
    mid = jnp.logical_and(owner == 1, slot < split)
    outer = jnp.logical_and(owner == 1, jnp.logical_and(slot >= split, jnp.logical_not(last)))

    weights = (wbp_hbm, wbg_hbm, wap_hbm, wag_hbm, wg_hbm, wo_hbm)
    loads = [pltpu.make_async_copy(pair_hbm, pair_v, in_sem.at[0])]
    for n, vector in enumerate((ngain_hbm, nbias_hbm, ogain_hbm, obias_hbm)):
        loads.append(pltpu.make_async_copy(vector, vec_v.at[n], in_sem.at[0]))
    for n, weight in enumerate(weights):
        span = w_v.at[:, n * hidden : (n + 1) * hidden]
        loads.append(pltpu.make_async_copy(weight, span, in_sem.at[1 if n < 2 else 2]))

    def loaded(span, index):
        pltpu.make_async_copy(span, span, in_sem.at[index]).wait()

    barrier = pltpu.get_barrier_semaphore()

    def greet(semaphore, target):
        pl.semaphore_signal(
            semaphore, inc=1, device_id=target, device_id_type=pl.DeviceIdType.MESH
        )

    left_copy = pltpu.make_async_remote_copy(
        src_ref=left_buf.at[sub],
        dst_ref=left_buf.at[sub],
        send_sem=in_sem.at[0],
        recv_sem=recv_sem.at[0],
        device_id={"sub": other},
        device_id_type=pl.DeviceIdType.MESH,
    )

    def block_copy(source, target_row, target_sub):
        return pltpu.make_async_remote_copy(
            src_ref=source,
            dst_ref=right_buf.at[2 * slot + sub],
            send_sem=send_sem,
            recv_sem=recv_sem.at[slot // split],
            device_id={"row": target_row, "sub": target_sub},
            device_id_type=pl.DeviceIdType.MESH,
        )

    raw_copy = block_copy(pair_hbm, 0, owner)
    copies = [block_copy(right_send, q, owner) for q in range(n_row)]
    sent = [jnp.logical_not(jnp.logical_and(near, row == q)) for q in range(n_row)]

    def start(first, end, guarded):
        for q in range(first, end):
            if guarded:

                @pl.when(sent[q])
                def _():
                    copies[q].start()
            else:
                copies[q].start()

    @pl.when(low_far)
    def _():
        greet(barrier, {"sub": 0})
        for step in range(half)[::-1]:
            greet(barrier, {"row": half + step, "sub": 0})
            if step >= split:
                greet(barrier, {"row": half + step, "sub": 1})

    @pl.when(high_near)
    def _():
        greet(barrier, {"sub": 0})
        for step in range(half):

            @pl.when(slot != step)
            def _():
                greet(barrier, {"row": half + step, "sub": 1})
                if step >= split:
                    greet(barrier, {"row": half + step, "sub": 0})

    @pl.when(last)
    def _():
        pl.semaphore_wait(barrier, 2 * half - sub)
        raw_copy.start()

        @pl.when(sub == 0)
        def _():
            greet(ready, {"sub": 1})
            for step in range(half):
                greet(late, {"row": step, "sub": 1})

    @pl.when(jnp.logical_and(high_far, jnp.logical_not(last)))
    def _():
        for step in range(half):
            greet(barrier, {"row": step, "sub": 1})

    @pl.when(low_near)
    def _():
        for step in range(1, half):
            greet(barrier, {"row": lax.rem(slot + step, half), "sub": 0})

    for load in loads:
        load.start()

    @pl.when(low_near)
    def _():
        pl.semaphore_wait(barrier, half)
        greet(ready, {"sub": 1})

    @pl.when(jnp.logical_and(high_far, mid))
    def _():
        pl.semaphore_wait(barrier, half + 1)
        greet(ready, {"sub": 1})

    loaded(bytes_v, 0)
    pair = pair_v[...].astype(jnp.float32).reshape(rows * cols, chan)
    centred, scale = centre(pair, vec_v[0])
    loaded(w_v.at[:, 0 : 2 * hidden], 1)
    right_shift = through(vec_v[1], w_v[:, 0 : 2 * hidden])
    right = gated(centred, scale, right_shift, w_v[:, 0 : 2 * hidden])
    right = right.reshape(rows, cols, hidden)
    right_send[...] = right

    @pl.when(low_far)
    def _():
        pl.semaphore_wait(ready, 1)

    @pl.when(jnp.logical_and(high_near, mid))
    def _():
        pl.semaphore_wait(ready, 1)

    @pl.when(outer)
    def _():
        pl.semaphore_wait(barrier, 2 * half - sub)

        @pl.when(sub == 0)
        def _():
            greet(ready, {"sub": 1})

    @pl.when(jnp.logical_and(sent[0], jnp.logical_not(last)))
    def _():
        copies[0].start()

    start(1, half, True)

    @pl.when(near)
    def _():
        right_buf[2 * slot + sub] = right

    loaded(w_v.at[:, 2 * hidden :], 2)
    left_shift = through(vec_v[1], w_v[:, 2 * hidden : 4 * hidden])
    left = gated(centred, scale, left_shift, w_v[:, 2 * hidden : 4 * hidden])
    left_buf[sub] = left.reshape(rows, cols, hidden)

    @pl.when(jnp.logical_and(high_near, jnp.logical_not(mid)))
    def _():
        pl.semaphore_wait(ready, 1)

    left_copy.start()

    @pl.when(jnp.logical_and(high_near, mid))
    def _():
        pl.semaphore_wait(barrier, half - 1)
        greet(ready, {"sub": 0})

    @pl.when(jnp.logical_and(high_far, mid))
    def _():
        pl.semaphore_wait(ready, 1)

    @pl.when(jnp.logical_not(low))
    def _():
        start(half, n_row, True)

    gate = w_v[:, 4 * hidden : 4 * hidden + chan]
    gating = jnp.dot(centred, gate, preferred_element_type=jnp.float32) * scale
    gating = sigmoid(gating + through(vec_v[1], gate)).astype(jnp.bfloat16)
    @pl.when(first)
    def _():
        gain = jnp.broadcast_to(vec_v[0], (chan, chan)).T[:, 0:1]
        folded = w_v[:, 0 : 2 * hidden].astype(jnp.float32) * gain
        folded = folded - jnp.mean(folded, axis=0, keepdims=True)
        high = folded.astype(jnp.bfloat16)
        fold_v[0:chan] = high
        fold_v[chan:] = (folded - high.astype(jnp.float32)).astype(jnp.bfloat16)

    w_out = w_v[:, 5 * hidden : 6 * hidden]
    out_shift = through(vec_v[3], w_out)

    @pl.when(low_far)
    def _():
        pl.semaphore_wait(barrier, half - 1)
        greet(ready, {"sub": 0})

    @pl.when(low_near)
    def _():
        pl.semaphore_wait(ready, 1)

    @pl.when(low)
    def _():
        for q in order:
            copies[q].start()
        pl.semaphore_wait(late, 1)

    @pl.when(low_far)
    def _():
        greet(late, {"sub": 0})

    @pl.when(low)
    def _():
        copies[-1].start()


    def arrived(group, blocks):
        pltpu.make_async_remote_copy(
            src_ref=right_buf.at[0:blocks],
            dst_ref=right_buf.at[0:blocks],
            send_sem=send_sem,
            recv_sem=recv_sem.at[group],
            device_id={"sub": other},
            device_id_type=pl.DeviceIdType.MESH,
        ).wait_recv()

    def block_of(source):
        return right_buf[2 * source : 2 * source + 2].astype(jnp.float32)

    def absorb(source, block):
        for i in range(rows):
            prod = left_buf[:, i].astype(jnp.float32)[:, None] * block
            prod = prod[0] + prod[1]
            prod = jnp.sum(prod.reshape(rows, cols // 8, 8, hidden), axis=1)
            tri_v[i, source * rows : (source + 1) * rows, :] = jnp.sum(prod, axis=1)

    def project(source):
        bits = right_buf[2 * source : 2 * source + 2].reshape(2 * rows * cols, chan)
        raw = bits.astype(jnp.float32)
        moved = raw - jnp.mean(raw, axis=-1, keepdims=True)
        raw_scale = lax.rsqrt(jnp.mean(moved * moved, axis=-1, keepdims=True) + EPSILON)
        twice = jnp.concatenate([bits, bits], axis=1)
        far = gated(twice, raw_scale, right_shift, fold_v[...])
        return far.astype(jnp.float32).reshape(2, rows, cols, hidden)


    for group in range(2):
        own = jnp.logical_and(near, slot // split == group)

        @pl.when(own)
        def _():
            arrived(group, 2 * split - group)

        @pl.when(jnp.logical_not(own))
        def _():
            arrived(group, 2 * split + 1 - group)

        if group == 1:

            @pl.when(first)
            def _():
                far = project(half - 1).astype(jnp.bfloat16)
                right_buf[2 * half - 2 :] = far

        for source in range(group * split, (group + 1) * split):
            absorb(source, block_of(source))

    tri = tri_v[...].reshape(rows * cols, hidden).astype(jnp.bfloat16).astype(jnp.float32)
    tri_centred, tri_scale = centre(tri, vec_v[2])
    mixed = jnp.dot(tri_centred, w_out, preferred_element_type=jnp.float32)
    mixed = mixed * tri_scale + out_shift
    out = (gating.astype(jnp.float32) * mixed).astype(jnp.bfloat16)
    out_ref[...] = out.reshape(rows, cols, chan)

    left_copy.wait_send()
    def gone(blocks):
        pltpu.make_async_remote_copy(
            src_ref=right_buf.at[0:blocks],
            dst_ref=right_buf.at[0:blocks],
            send_sem=send_sem,
            recv_sem=recv_sem.at[0],
            device_id={"sub": other},
            device_id_type=pl.DeviceIdType.MESH,
        ).wait_send()

    @pl.when(near)
    def _():
        gone(n_row - 1)

    @pl.when(jnp.logical_not(near))
    def _():
        gone(n_row)


def one_round(n_row, pair_rep, norm_gain, norm_bias, *rest):
    w_a_proj, w_a_gate, w_b_proj, w_b_gate, w_gate, out_gain, out_bias, w_out = rest
    rows, cols, chan = pair_rep.shape
    hidden = w_a_proj.shape[1]
    half = n_row // 2
    hbm = pl.BlockSpec(memory_space=pltpu.HBM)
    return pl.pallas_call(
        functools.partial(kernel, n_row),
        out_shape=pltpu.VMEM((rows, cols, chan), jnp.bfloat16),
        in_specs=[hbm] * 11,
        out_specs=pl.BlockSpec(memory_space=pltpu.VMEM),
        scratch_shapes=[
            pltpu.VMEM((rows, cols, chan), jnp.bfloat16),
            pltpu.VMEM((4, 1, chan), jnp.float32),
            pltpu.VMEM((chan, 6 * hidden), jnp.bfloat16),
            pltpu.VMEM((rows, cols, hidden), jnp.bfloat16),
            pltpu.VMEM((2 * half, rows, cols, hidden), jnp.bfloat16),
            pltpu.VMEM((2, rows, cols, hidden), jnp.bfloat16),
            pltpu.VMEM((rows, cols, hidden), jnp.float32),
            pltpu.SemaphoreType.DMA((3,)),
            pltpu.SemaphoreType.DMA,
            pltpu.SemaphoreType.DMA((2,)),
            pltpu.SemaphoreType.REGULAR,
            pltpu.SemaphoreType.REGULAR,
            pltpu.VMEM((rows * cols // 2 + 4, 1, chan), jnp.float32),
            pltpu.VMEM((2 * chan, 2 * hidden), jnp.bfloat16),
        ],
        compiler_params=pltpu.CompilerParams(
            collective_id=0, has_side_effects=True, vmem_limit_bytes=16 * 2**20
        ),
    )(
        *(
            pltpu.with_memory_space_constraint(operand, pltpu.HBM)
            for operand in (
                pair_rep,
                norm_gain.reshape(1, chan),
                norm_bias.reshape(1, chan),
                w_a_proj,
                w_a_gate,
                w_b_proj,
                w_b_gate,
                w_gate,
                out_gain.reshape(1, hidden),
                out_bias.reshape(1, hidden),
                w_out,
            )
        )
    )


def body(n_row, n_sub, *operands):
    rows, cols, chan = operands[0].shape
    hidden = operands[3].shape[1]
    gathered = cols * cols * n_sub * hidden * 2
    if n_sub == 2 and n_row % 4 == 0 and cols % 16 == 0 and hidden == chan and gathered <= 4 * 2**20:
        return one_round(n_row, *operands)
    return per_device(*operands)


def solution(mesh):
    in_specs = (P(("grp", "row"), "sub", None), P(), P(), P(), P(), P(), P(), P(), P(), P(), P())
    out_specs = P(("grp", "row"), "sub", None)
    return jax.shard_map(
        functools.partial(body, mesh.shape["row"], mesh.shape["sub"]),
        mesh=mesh,
        in_specs=in_specs,
        out_specs=out_specs,
        check_vma=False,
    )
```

```python
import functools

import jax
import jax.numpy as jnp
from jax import lax
from jax.experimental import pallas as pl
from jax.experimental.pallas import tpu as pltpu
from jax.sharding import PartitionSpec as P

EPSILON = 1e-05


def layer_norm(values, gain, shift, axis):
    centred = values - jnp.mean(values, axis=axis, keepdims=True)
    variance = jnp.mean(centred * centred, axis=axis, keepdims=True)
    return centred * lax.rsqrt(variance + EPSILON) * gain + shift


def per_device(
    pair_rep,
    norm_gain,
    norm_bias,
    w_a_proj,
    w_a_gate,
    w_b_proj,
    w_b_gate,
    w_gate,
    out_gain,
    out_bias,
    w_out,
):
    hidden = w_a_proj.shape[1]
    w_inner = jnp.concatenate([w_a_proj, w_a_gate, w_b_proj, w_b_gate], axis=1)
    normed = layer_norm(pair_rep.astype(jnp.float32), norm_gain, norm_bias, -1).astype(jnp.bfloat16)
    inner = jnp.einsum("rkc,cm->mrk", normed, w_inner, preferred_element_type=jnp.float32)
    left_local = (jax.nn.sigmoid(inner[hidden : 2 * hidden]) * inner[:hidden]).astype(jnp.bfloat16)
    right_local = (
        jax.nn.sigmoid(inner[3 * hidden : 4 * hidden]) * inner[2 * hidden : 3 * hidden]
    ).astype(jnp.bfloat16)
    gating = jax.nn.sigmoid(
        jnp.einsum("rkc,cd->rkd", normed, w_gate, preferred_element_type=jnp.float32)
    ).astype(jnp.bfloat16)
    left_chan, right_chan = (
        lax.all_to_all(left_local, "row", split_axis=0, concat_axis=1, tiled=True),
        lax.all_to_all(right_local, "row", split_axis=0, concat_axis=1, tiled=True),
    )
    left_rows = lax.all_to_all(left_chan, "sub", split_axis=1, concat_axis=2, tiled=True)
    triangle = jnp.einsum(
        "hik,hjk->hij",
        left_rows,
        lax.all_gather(right_chan, "sub", axis=2, tiled=True),
        preferred_element_type=jnp.float32,
    ).astype(jnp.bfloat16)
    regrouped = lax.all_to_all(
        lax.all_to_all(triangle, "sub", split_axis=2, concat_axis=1, tiled=True),
        "row",
        split_axis=1,
        concat_axis=0,
        tiled=True,
    )
    hidden_normed = layer_norm(
        regrouped.astype(jnp.float32), out_gain[:, None, None], out_bias[:, None, None], 0
    ).astype(jnp.bfloat16)
    mixed = jnp.einsum("hrj,hc->rjc", hidden_normed, w_out, preferred_element_type=jnp.float32)
    return (gating.astype(jnp.float32) * mixed).astype(jnp.bfloat16)


def sigmoid(values):
    return 0.5 * jnp.tanh(0.5 * values) + 0.5


def centre(values, gain):
    centred = values - jnp.mean(values, axis=-1, keepdims=True)
    scale = lax.rsqrt(jnp.mean(centred * centred, axis=-1, keepdims=True) + EPSILON)
    return (centred * gain).astype(jnp.bfloat16), scale


def through(shift, weights):
    high = shift.astype(jnp.bfloat16)
    low = (shift - high.astype(jnp.float32)).astype(jnp.bfloat16)
    pair = jnp.concatenate([jnp.broadcast_to(high, (8, high.shape[1])), jnp.broadcast_to(low, (8, low.shape[1]))], axis=0)
    mixed = jnp.dot(pair, weights, preferred_element_type=jnp.float32)
    return mixed[0:1] + mixed[8:9]


def gated(centred, scale, shift, weights):
    hidden = weights.shape[1] // 2
    inner = jnp.dot(centred, weights, preferred_element_type=jnp.float32) * scale + shift
    return (sigmoid(inner[:, hidden:]) * inner[:, :hidden]).astype(jnp.bfloat16)


def kernel(
    n_row,
    pair_hbm,
    ngain_hbm,
    nbias_hbm,
    wap_hbm,
    wag_hbm,
    wbp_hbm,
    wbg_hbm,
    wg_hbm,
    ogain_hbm,
    obias_hbm,
    wo_hbm,
    out_ref,
    pair_v,
    vec_v,
    w_v,
    right_send,
    right_buf,
    left_buf,
    tri_v,
    in_sem,
    send_sem,
    recv_sem,
    ready,
    late,
    bytes_v,
    fold_v,
):
    rows, cols, chan = pair_v.shape
    hidden = right_send.shape[-1]
    half = n_row // 2
    row = lax.axis_index("row")
    sub = lax.axis_index("sub")
    other = 1 - sub
    owner = row // half
    slot = lax.rem(row, half)
    near = sub == owner
    low = owner == 0
    low_near = jnp.logical_and(low, sub == 0)
    low_far = jnp.logical_and(low, sub == 1)
    high_near = jnp.logical_and(owner == 1, sub == 1)
    high_far = jnp.logical_and(owner == 1, sub == 0)
    last = row == n_row - 1
    first = jnp.logical_and(low_far, row == 0)
    split = half // 2
    order = [half + q for pair in zip(range(split), range(split, half - 1)) for q in pair]
    order += [q for q in range(half, n_row - 1) if q not in order]
    mid = jnp.logical_and(owner == 1, slot < split)
    outer = jnp.logical_and(owner == 1, jnp.logical_and(slot >= split, jnp.logical_not(last)))

    weights = (wbp_hbm, wbg_hbm, wap_hbm, wag_hbm, wg_hbm, wo_hbm)
    loads = [pltpu.make_async_copy(pair_hbm, pair_v, in_sem.at[0])]
    for n, vector in enumerate((ngain_hbm, nbias_hbm, ogain_hbm, obias_hbm)):
        loads.append(pltpu.make_async_copy(vector, vec_v.at[n], in_sem.at[0]))
    for n, weight in enumerate(weights):
        span = w_v.at[:, n * hidden : (n + 1) * hidden]
        loads.append(pltpu.make_async_copy(weight, span, in_sem.at[1 if n < 2 else 2]))

    def loaded(span, index):
        pltpu.make_async_copy(span, span, in_sem.at[index]).wait()

    barrier = pltpu.get_barrier_semaphore()

    def greet(semaphore, target):
        pl.semaphore_signal(
            semaphore, inc=1, device_id=target, device_id_type=pl.DeviceIdType.MESH
        )

    left_copy = pltpu.make_async_remote_copy(
        src_ref=left_buf.at[sub],
        dst_ref=left_buf.at[sub],
        send_sem=in_sem.at[0],
        recv_sem=recv_sem.at[0],
        device_id={"sub": other},
        device_id_type=pl.DeviceIdType.MESH,
    )

    def block_copy(source, target_row, target_sub):
        return pltpu.make_async_remote_copy(
            src_ref=source,
            dst_ref=right_buf.at[2 * slot + sub],
            send_sem=send_sem,
            recv_sem=recv_sem.at[slot // split],
            device_id={"row": target_row, "sub": target_sub},
            device_id_type=pl.DeviceIdType.MESH,
        )

    raw_copy = block_copy(pair_hbm, 0, owner)
    copies = [block_copy(right_send, q, owner) for q in range(n_row)]
    sent = [jnp.logical_not(jnp.logical_and(near, row == q)) for q in range(n_row)]

    def start(first, end, guarded):
        for q in range(first, end):
            if guarded:

                @pl.when(sent[q])
                def _():
                    copies[q].start()
            else:
                copies[q].start()

    @pl.when(low_far)
    def _():
        greet(barrier, {"sub": 0})
        for step in range(half)[::-1]:
            greet(barrier, {"row": half + step, "sub": 0})
            if step >= split:
                greet(barrier, {"row": half + step, "sub": 1})

    @pl.when(high_near)
    def _():
        greet(barrier, {"sub": 0})
        for step in range(half):

            @pl.when(slot != step)
            def _():
                greet(barrier, {"row": half + step, "sub": 1})
                if step >= split:
                    greet(barrier, {"row": half + step, "sub": 0})

    @pl.when(last)
    def _():
        pl.semaphore_wait(barrier, 2 * half - sub)
        raw_copy.start()

        @pl.when(sub == 0)
        def _():
            greet(ready, {"sub": 1})
            for step in range(half):
                greet(late, {"row": step, "sub": 1})

    @pl.when(jnp.logical_and(high_far, jnp.logical_not(last)))
    def _():
        for step in range(half):
            greet(barrier, {"row": step, "sub": 1})

    @pl.when(low_near)
    def _():
        for step in range(1, half):
            greet(barrier, {"row": lax.rem(slot + step, half), "sub": 0})

    for load in loads:
        load.start()

    @pl.when(low_near)
    def _():
        pl.semaphore_wait(barrier, half)
        greet(ready, {"sub": 1})

    @pl.when(jnp.logical_and(high_far, mid))
    def _():
        pl.semaphore_wait(barrier, half + 1)
        greet(ready, {"sub": 1})

    loaded(bytes_v, 0)
    pair = pair_v[...].astype(jnp.float32).reshape(rows * cols, chan)
    centred, scale = centre(pair, vec_v[0])
    loaded(w_v.at[:, 0 : 2 * hidden], 1)
    right_shift = through(vec_v[1], w_v[:, 0 : 2 * hidden])
    right = gated(centred, scale, right_shift, w_v[:, 0 : 2 * hidden])
    right = right.reshape(rows, cols, hidden)
    right_send[...] = right

    @pl.when(low_far)
    def _():
        pl.semaphore_wait(ready, 1)

    @pl.when(jnp.logical_and(high_near, mid))
    def _():
        pl.semaphore_wait(ready, 1)

    @pl.when(outer)
    def _():
        pl.semaphore_wait(barrier, 2 * half - sub)

        @pl.when(sub == 0)
        def _():
            greet(ready, {"sub": 1})

    @pl.when(jnp.logical_and(sent[0], jnp.logical_not(last)))
    def _():
        copies[0].start()

    start(1, half, True)

    @pl.when(near)
    def _():
        right_buf[2 * slot + sub] = right

    loaded(w_v.at[:, 2 * hidden :], 2)
    left_shift = through(vec_v[1], w_v[:, 2 * hidden : 4 * hidden])
    left = gated(centred, scale, left_shift, w_v[:, 2 * hidden : 4 * hidden])
    left_buf[sub] = left.reshape(rows, cols, hidden)

    @pl.when(jnp.logical_and(high_near, jnp.logical_not(mid)))
    def _():
        pl.semaphore_wait(ready, 1)

    left_copy.start()

    @pl.when(jnp.logical_and(high_near, mid))
    def _():
        pl.semaphore_wait(barrier, half - 1)
        greet(ready, {"sub": 0})

    @pl.when(jnp.logical_and(high_far, mid))
    def _():
        pl.semaphore_wait(ready, 1)

    @pl.when(jnp.logical_not(low))
    def _():
        start(half, n_row, True)

    gate = w_v[:, 4 * hidden : 4 * hidden + chan]
    gating = jnp.dot(centred, gate, preferred_element_type=jnp.float32) * scale
    gating = sigmoid(gating + through(vec_v[1], gate)).astype(jnp.bfloat16)
    @pl.when(first)
    def _():
        gain = jnp.broadcast_to(vec_v[0], (chan, chan)).T[:, 0:1]
        folded = w_v[:, 0 : 2 * hidden].astype(jnp.float32) * gain
        folded = folded - jnp.mean(folded, axis=0, keepdims=True)
        high = folded.astype(jnp.bfloat16)
        fold_v[0:chan] = high
        fold_v[chan:] = (folded - high.astype(jnp.float32)).astype(jnp.bfloat16)

    w_out = w_v[:, 5 * hidden : 6 * hidden]
    out_shift = through(vec_v[3], w_out)

    @pl.when(low_far)
    def _():
        pl.semaphore_wait(barrier, half - 1)
        greet(ready, {"sub": 0})

    @pl.when(low_near)
    def _():
        pl.semaphore_wait(ready, 1)

    @pl.when(low)
    def _():
        for q in order:
            copies[q].start()
        pl.semaphore_wait(late, 1)

    @pl.when(low_far)
    def _():
        greet(late, {"sub": 0})

    @pl.when(low)
    def _():
        copies[-1].start()


    def arrived(group, blocks):
        pltpu.make_async_remote_copy(
            src_ref=right_buf.at[0:blocks],
            dst_ref=right_buf.at[0:blocks],
            send_sem=send_sem,
            recv_sem=recv_sem.at[group],
            device_id={"sub": other},
            device_id_type=pl.DeviceIdType.MESH,
        ).wait_recv()

    def block_of(source):
        return right_buf[2 * source : 2 * source + 2].astype(jnp.float32)

    def absorb(source, block):
        for i in range(rows):
            prod = left_buf[:, i].astype(jnp.float32)[:, None] * block
            prod = prod[0] + prod[1]
            prod = jnp.sum(prod.reshape(rows, cols // 8, 8, hidden), axis=1)
            tri_v[i, source * rows : (source + 1) * rows, :] = jnp.sum(prod, axis=1)

    def project(source):
        bits = right_buf[2 * source : 2 * source + 2].reshape(2 * rows * cols, chan)
        raw = bits.astype(jnp.float32)
        moved = raw - jnp.mean(raw, axis=-1, keepdims=True)
        raw_scale = lax.rsqrt(jnp.mean(moved * moved, axis=-1, keepdims=True) + EPSILON)
        twice = jnp.concatenate([bits, bits], axis=1)
        far = gated(twice, raw_scale, right_shift, fold_v[...])
        return far.astype(jnp.float32).reshape(2, rows, cols, hidden)


    for group in range(2):
        own = jnp.logical_and(near, slot // split == group)

        @pl.when(own)
        def _():
            arrived(group, 2 * split - group)

        @pl.when(jnp.logical_not(own))
        def _():
            arrived(group, 2 * split + 1 - group)

        if group == 1:

            @pl.when(first)
            def _():
                far = project(half - 1).astype(jnp.bfloat16)
                right_buf[2 * half - 2 :] = far

        whole = right_buf[2 * group * split : 2 * (group + 1) * split].astype(jnp.float32)
        whole = whole.reshape(split, 2, rows, cols // 8, 8, hidden)
        for i in range(rows):
            mine = left_buf[:, i].astype(jnp.float32).reshape(1, 2, 1, cols // 8, 8, hidden)
            prod = jnp.sum(jnp.sum(mine * whole, axis=3), axis=1)
            prod = jnp.sum(prod, axis=2).reshape(split * rows, hidden)
            tri_v[i, group * split * rows : (group + 1) * split * rows, :] = prod

    tri = tri_v[...].reshape(rows * cols, hidden).astype(jnp.bfloat16).astype(jnp.float32)
    tri_centred, tri_scale = centre(tri, vec_v[2])
    mixed = jnp.dot(tri_centred, w_out, preferred_element_type=jnp.float32)
    mixed = mixed * tri_scale + out_shift
    out = (gating.astype(jnp.float32) * mixed).astype(jnp.bfloat16)
    out_ref[...] = out.reshape(rows, cols, chan)

    left_copy.wait_send()
    def gone(blocks):
        pltpu.make_async_remote_copy(
            src_ref=right_buf.at[0:blocks],
            dst_ref=right_buf.at[0:blocks],
            send_sem=send_sem,
            recv_sem=recv_sem.at[0],
            device_id={"sub": other},
            device_id_type=pl.DeviceIdType.MESH,
        ).wait_send()

    @pl.when(near)
    def _():
        gone(n_row - 1)

    @pl.when(jnp.logical_not(near))
    def _():
        gone(n_row)


def one_round(n_row, pair_rep, norm_gain, norm_bias, *rest):
    w_a_proj, w_a_gate, w_b_proj, w_b_gate, w_gate, out_gain, out_bias, w_out = rest
    rows, cols, chan = pair_rep.shape
    hidden = w_a_proj.shape[1]
    half = n_row // 2
    hbm = pl.BlockSpec(memory_space=pltpu.HBM)
    return pl.pallas_call(
        functools.partial(kernel, n_row),
        out_shape=pltpu.VMEM((rows, cols, chan), jnp.bfloat16),
        in_specs=[hbm] * 11,
        out_specs=pl.BlockSpec(memory_space=pltpu.VMEM),
        scratch_shapes=[
            pltpu.VMEM((rows, cols, chan), jnp.bfloat16),
            pltpu.VMEM((4, 1, chan), jnp.float32),
            pltpu.VMEM((chan, 6 * hidden), jnp.bfloat16),
            pltpu.VMEM((rows, cols, hidden), jnp.bfloat16),
            pltpu.VMEM((2 * half, rows, cols, hidden), jnp.bfloat16),
            pltpu.VMEM((2, rows, cols, hidden), jnp.bfloat16),
            pltpu.VMEM((rows, cols, hidden), jnp.float32),
            pltpu.SemaphoreType.DMA((3,)),
            pltpu.SemaphoreType.DMA,
            pltpu.SemaphoreType.DMA((2,)),
            pltpu.SemaphoreType.REGULAR,
            pltpu.SemaphoreType.REGULAR,
            pltpu.VMEM((rows * cols // 2 + 4, 1, chan), jnp.float32),
            pltpu.VMEM((2 * chan, 2 * hidden), jnp.bfloat16),
        ],
        compiler_params=pltpu.CompilerParams(
            collective_id=0, has_side_effects=True, vmem_limit_bytes=16 * 2**20
        ),
    )(
        *(
            pltpu.with_memory_space_constraint(operand, pltpu.HBM)
            for operand in (
                pair_rep,
                norm_gain.reshape(1, chan),
                norm_bias.reshape(1, chan),
                w_a_proj,
                w_a_gate,
                w_b_proj,
                w_b_gate,
                w_gate,
                out_gain.reshape(1, hidden),
                out_bias.reshape(1, hidden),
                w_out,
            )
        )
    )


def body(n_row, n_sub, *operands):
    rows, cols, chan = operands[0].shape
    hidden = operands[3].shape[1]
    gathered = cols * cols * n_sub * hidden * 2
    if n_sub == 2 and n_row % 4 == 0 and cols % 16 == 0 and hidden == chan and gathered <= 4 * 2**20:
        return one_round(n_row, *operands)
    return per_device(*operands)


def solution(mesh):
    in_specs = (P(("grp", "row"), "sub", None), P(), P(), P(), P(), P(), P(), P(), P(), P(), P())
    out_specs = P(("grp", "row"), "sub", None)
    return jax.shard_map(
        functools.partial(body, mesh.shape["row"], mesh.shape["sub"]),
        mesh=mesh,
        in_specs=in_specs,
        out_specs=out_specs,
        check_vma=False,
    )
```

```python
import functools

import jax
import jax.numpy as jnp
from jax import lax
from jax.experimental import pallas as pl
from jax.experimental.pallas import tpu as pltpu
from jax.sharding import PartitionSpec as P

EPSILON = 1e-05


def layer_norm(values, gain, shift, axis):
    centred = values - jnp.mean(values, axis=axis, keepdims=True)
    variance = jnp.mean(centred * centred, axis=axis, keepdims=True)
    return centred * lax.rsqrt(variance + EPSILON) * gain + shift


def per_device(
    pair_rep,
    norm_gain,
    norm_bias,
    w_a_proj,
    w_a_gate,
    w_b_proj,
    w_b_gate,
    w_gate,
    out_gain,
    out_bias,
    w_out,
):
    hidden = w_a_proj.shape[1]
    w_inner = jnp.concatenate([w_a_proj, w_a_gate, w_b_proj, w_b_gate], axis=1)
    normed = layer_norm(pair_rep.astype(jnp.float32), norm_gain, norm_bias, -1).astype(jnp.bfloat16)
    inner = jnp.einsum("rkc,cm->mrk", normed, w_inner, preferred_element_type=jnp.float32)
    left_local = (jax.nn.sigmoid(inner[hidden : 2 * hidden]) * inner[:hidden]).astype(jnp.bfloat16)
    right_local = (
        jax.nn.sigmoid(inner[3 * hidden : 4 * hidden]) * inner[2 * hidden : 3 * hidden]
    ).astype(jnp.bfloat16)
    gating = jax.nn.sigmoid(
        jnp.einsum("rkc,cd->rkd", normed, w_gate, preferred_element_type=jnp.float32)
    ).astype(jnp.bfloat16)
    left_chan, right_chan = (
        lax.all_to_all(left_local, "row", split_axis=0, concat_axis=1, tiled=True),
        lax.all_to_all(right_local, "row", split_axis=0, concat_axis=1, tiled=True),
    )
    left_rows = lax.all_to_all(left_chan, "sub", split_axis=1, concat_axis=2, tiled=True)
    triangle = jnp.einsum(
        "hik,hjk->hij",
        left_rows,
        lax.all_gather(right_chan, "sub", axis=2, tiled=True),
        preferred_element_type=jnp.float32,
    ).astype(jnp.bfloat16)
    regrouped = lax.all_to_all(
        lax.all_to_all(triangle, "sub", split_axis=2, concat_axis=1, tiled=True),
        "row",
        split_axis=1,
        concat_axis=0,
        tiled=True,
    )
    hidden_normed = layer_norm(
        regrouped.astype(jnp.float32), out_gain[:, None, None], out_bias[:, None, None], 0
    ).astype(jnp.bfloat16)
    mixed = jnp.einsum("hrj,hc->rjc", hidden_normed, w_out, preferred_element_type=jnp.float32)
    return (gating.astype(jnp.float32) * mixed).astype(jnp.bfloat16)


def sigmoid(values):
    return 0.5 * jnp.tanh(0.5 * values) + 0.5


def centre(values, gain):
    centred = values - jnp.mean(values, axis=-1, keepdims=True)
    scale = lax.rsqrt(jnp.mean(centred * centred, axis=-1, keepdims=True) + EPSILON)
    return (centred * gain).astype(jnp.bfloat16), scale


def through(shift, weights):
    high = shift.astype(jnp.bfloat16)
    low = (shift - high.astype(jnp.float32)).astype(jnp.bfloat16)
    pair = jnp.concatenate([jnp.broadcast_to(high, (8, high.shape[1])), jnp.broadcast_to(low, (8, low.shape[1]))], axis=0)
    mixed = jnp.dot(pair, weights, preferred_element_type=jnp.float32)
    return mixed[0:1] + mixed[8:9]


def gated(centred, scale, shift, weights):
    hidden = weights.shape[1] // 2
    inner = jnp.dot(centred, weights, preferred_element_type=jnp.float32) * scale + shift
    return (sigmoid(inner[:, hidden:]) * inner[:, :hidden]).astype(jnp.bfloat16)


def kernel(
    n_row,
    pair_hbm,
    ngain_hbm,
    nbias_hbm,
    wap_hbm,
    wag_hbm,
    wbp_hbm,
    wbg_hbm,
    wg_hbm,
    ogain_hbm,
    obias_hbm,
    wo_hbm,
    out_ref,
    pair_v,
    vec_v,
    w_v,
    right_send,
    right_buf,
    left_buf,
    tri_v,
    in_sem,
    send_sem,
    recv_sem,
    ready,
    late,
    bytes_v,
    fold_v,
):
    rows, cols, chan = pair_v.shape
    hidden = right_send.shape[-1]
    half = n_row // 2
    row = lax.axis_index("row")
    sub = lax.axis_index("sub")
    other = 1 - sub
    owner = row // half
    slot = lax.rem(row, half)
    near = sub == owner
    low = owner == 0
    low_near = jnp.logical_and(low, sub == 0)
    low_far = jnp.logical_and(low, sub == 1)
    high_near = jnp.logical_and(owner == 1, sub == 1)
    high_far = jnp.logical_and(owner == 1, sub == 0)
    last = row == n_row - 1
    first = jnp.logical_and(low_far, row == 0)
    split = half // 2
    order = [half + q for pair in zip(range(split), range(split, half - 1)) for q in pair]
    order += [q for q in range(half, n_row - 1) if q not in order]
    mid = jnp.logical_and(owner == 1, slot < split)
    outer = jnp.logical_and(owner == 1, jnp.logical_and(slot >= split, jnp.logical_not(last)))

    weights = (wbp_hbm, wbg_hbm, wap_hbm, wag_hbm, wg_hbm, wo_hbm)
    loads = [pltpu.make_async_copy(pair_hbm, pair_v, in_sem.at[0])]
    for n, vector in enumerate((ngain_hbm, nbias_hbm, ogain_hbm, obias_hbm)):
        loads.append(pltpu.make_async_copy(vector, vec_v.at[n], in_sem.at[0]))
    for n, weight in enumerate(weights):
        span = w_v.at[:, n * hidden : (n + 1) * hidden]
        loads.append(pltpu.make_async_copy(weight, span, in_sem.at[1]))

    def loaded(span, index):
        pltpu.make_async_copy(span, span, in_sem.at[index]).wait()

    barrier = pltpu.get_barrier_semaphore()

    def greet(semaphore, target):
        pl.semaphore_signal(
            semaphore, inc=1, device_id=target, device_id_type=pl.DeviceIdType.MESH
        )

    left_copy = pltpu.make_async_remote_copy(
        src_ref=left_buf.at[sub],
        dst_ref=left_buf.at[sub],
        send_sem=in_sem.at[0],
        recv_sem=recv_sem.at[0],
        device_id={"sub": other},
        device_id_type=pl.DeviceIdType.MESH,
    )

    def block_copy(source, target_row, target_sub):
        return pltpu.make_async_remote_copy(
            src_ref=source,
            dst_ref=right_buf.at[2 * slot + sub],
            send_sem=send_sem,
            recv_sem=recv_sem.at[slot // split],
            device_id={"row": target_row, "sub": target_sub},
            device_id_type=pl.DeviceIdType.MESH,
        )

    raw_copy = block_copy(pair_hbm, 0, owner)
    copies = [block_copy(right_send, q, owner) for q in range(n_row)]
    sent = [jnp.logical_not(jnp.logical_and(near, row == q)) for q in range(n_row)]

    def start(first, end, guarded):
        for q in range(first, end):
            if guarded:

                @pl.when(sent[q])
                def _():
                    copies[q].start()
            else:
                copies[q].start()

    @pl.when(low_far)
    def _():
        greet(barrier, {"sub": 0})
        for step in range(half)[::-1]:
            greet(barrier, {"row": half + step, "sub": 0})
            if step >= split:
                greet(barrier, {"row": half + step, "sub": 1})

    @pl.when(high_near)
    def _():
        greet(barrier, {"sub": 0})
        for step in range(half):

            @pl.when(slot != step)
            def _():
                greet(barrier, {"row": half + step, "sub": 1})
                if step >= split:
                    greet(barrier, {"row": half + step, "sub": 0})

    @pl.when(last)
    def _():
        pl.semaphore_wait(barrier, 2 * half - sub)
        raw_copy.start()

        @pl.when(sub == 0)
        def _():
            greet(ready, {"sub": 1})
            for step in range(half):
                greet(late, {"row": step, "sub": 1})

    @pl.when(jnp.logical_and(high_far, jnp.logical_not(last)))
    def _():
        for step in range(half):
            greet(barrier, {"row": step, "sub": 1})

    @pl.when(low_near)
    def _():
        for step in range(1, half):
            greet(barrier, {"row": lax.rem(slot + step, half), "sub": 0})

    for load in loads:
        load.start()

    @pl.when(low_near)
    def _():
        pl.semaphore_wait(barrier, half)
        greet(ready, {"sub": 1})

    @pl.when(jnp.logical_and(high_far, mid))
    def _():
        pl.semaphore_wait(barrier, half + 1)
        greet(ready, {"sub": 1})

    loaded(bytes_v, 0)
    pair = pair_v[...].astype(jnp.float32).reshape(rows * cols, chan)
    centred, scale = centre(pair, vec_v[0])
    loaded(w_v, 1)
    right_shift = through(vec_v[1], w_v[:, 0 : 2 * hidden])
    right = gated(centred, scale, right_shift, w_v[:, 0 : 2 * hidden])
    right = right.reshape(rows, cols, hidden)
    right_send[...] = right

    @pl.when(low_far)
    def _():
        pl.semaphore_wait(ready, 1)

    @pl.when(jnp.logical_and(high_near, mid))
    def _():
        pl.semaphore_wait(ready, 1)

    @pl.when(outer)
    def _():
        pl.semaphore_wait(barrier, 2 * half - sub)

        @pl.when(sub == 0)
        def _():
            greet(ready, {"sub": 1})

    @pl.when(jnp.logical_and(sent[0], jnp.logical_not(last)))
    def _():
        copies[0].start()

    start(1, half, True)

    @pl.when(near)
    def _():
        right_buf[2 * slot + sub] = right

    left_shift = through(vec_v[1], w_v[:, 2 * hidden : 4 * hidden])
    left = gated(centred, scale, left_shift, w_v[:, 2 * hidden : 4 * hidden])
    left_buf[sub] = left.reshape(rows, cols, hidden)

    @pl.when(jnp.logical_and(high_near, jnp.logical_not(mid)))
    def _():
        pl.semaphore_wait(ready, 1)

    left_copy.start()

    @pl.when(jnp.logical_and(high_near, mid))
    def _():
        pl.semaphore_wait(barrier, half - 1)
        greet(ready, {"sub": 0})

    @pl.when(jnp.logical_and(high_far, mid))
    def _():
        pl.semaphore_wait(ready, 1)

    @pl.when(jnp.logical_not(low))
    def _():
        start(half, n_row, True)

    gate = w_v[:, 4 * hidden : 4 * hidden + chan]
    gating = jnp.dot(centred, gate, preferred_element_type=jnp.float32) * scale
    gating = sigmoid(gating + through(vec_v[1], gate)).astype(jnp.bfloat16)
    @pl.when(first)
    def _():
        gain = jnp.broadcast_to(vec_v[0], (chan, chan)).T[:, 0:1]
        folded = w_v[:, 0 : 2 * hidden].astype(jnp.float32) * gain
        folded = folded - jnp.mean(folded, axis=0, keepdims=True)
        high = folded.astype(jnp.bfloat16)
        fold_v[0:chan] = high
        fold_v[chan:] = (folded - high.astype(jnp.float32)).astype(jnp.bfloat16)

    w_out = w_v[:, 5 * hidden : 6 * hidden]
    out_shift = through(vec_v[3], w_out)

    @pl.when(low_far)
    def _():
        pl.semaphore_wait(barrier, half - 1)
        greet(ready, {"sub": 0})

    @pl.when(low_near)
    def _():
        pl.semaphore_wait(ready, 1)

    @pl.when(low)
    def _():
        for q in order:
            copies[q].start()
        pl.semaphore_wait(late, 1)

    @pl.when(low_far)
    def _():
        greet(late, {"sub": 0})

    @pl.when(low)
    def _():
        copies[-1].start()


    def arrived(group, blocks):
        pltpu.make_async_remote_copy(
            src_ref=right_buf.at[0:blocks],
            dst_ref=right_buf.at[0:blocks],
            send_sem=send_sem,
            recv_sem=recv_sem.at[group],
            device_id={"sub": other},
            device_id_type=pl.DeviceIdType.MESH,
        ).wait_recv()

    def block_of(source):
        return right_buf[2 * source : 2 * source + 2].astype(jnp.float32)

    def absorb(source, block):
        for i in range(rows):
            prod = left_buf[:, i].astype(jnp.float32)[:, None] * block
            prod = prod[0] + prod[1]
            prod = jnp.sum(prod.reshape(rows, cols // 8, 8, hidden), axis=1)
            tri_v[i, source * rows : (source + 1) * rows, :] = jnp.sum(prod, axis=1)

    def project(source):
        bits = right_buf[2 * source : 2 * source + 2].reshape(2 * rows * cols, chan)
        raw = bits.astype(jnp.float32)
        moved = raw - jnp.mean(raw, axis=-1, keepdims=True)
        raw_scale = lax.rsqrt(jnp.mean(moved * moved, axis=-1, keepdims=True) + EPSILON)
        twice = jnp.concatenate([bits, bits], axis=1)
        far = gated(twice, raw_scale, right_shift, fold_v[...])
        return far.astype(jnp.float32).reshape(2, rows, cols, hidden)


    for group in range(2):
        own = jnp.logical_and(near, slot // split == group)

        @pl.when(own)
        def _():
            arrived(group, 2 * split - group)

        @pl.when(jnp.logical_not(own))
        def _():
            arrived(group, 2 * split + 1 - group)

        if group == 1:

            @pl.when(first)
            def _():
                far = project(half - 1).astype(jnp.bfloat16)
                right_buf[2 * half - 2 :] = far

        for source in range(group * split, (group + 1) * split):
            absorb(source, block_of(source))

    tri = tri_v[...].reshape(rows * cols, hidden).astype(jnp.bfloat16).astype(jnp.float32)
    tri_centred, tri_scale = centre(tri, vec_v[2])
    mixed = jnp.dot(tri_centred, w_out, preferred_element_type=jnp.float32)
    mixed = mixed * tri_scale + out_shift
    out = (gating.astype(jnp.float32) * mixed).astype(jnp.bfloat16)
    out_ref[...] = out.reshape(rows, cols, chan)

    left_copy.wait_send()
    def gone(blocks):
        pltpu.make_async_remote_copy(
            src_ref=right_buf.at[0:blocks],
            dst_ref=right_buf.at[0:blocks],
            send_sem=send_sem,
            recv_sem=recv_sem.at[0],
            device_id={"sub": other},
            device_id_type=pl.DeviceIdType.MESH,
        ).wait_send()

    @pl.when(near)
    def _():
        gone(n_row - 1)

    @pl.when(jnp.logical_not(near))
    def _():
        gone(n_row)


def one_round(n_row, pair_rep, norm_gain, norm_bias, *rest):
    w_a_proj, w_a_gate, w_b_proj, w_b_gate, w_gate, out_gain, out_bias, w_out = rest
    rows, cols, chan = pair_rep.shape
    hidden = w_a_proj.shape[1]
    half = n_row // 2
    hbm = pl.BlockSpec(memory_space=pltpu.HBM)
    return pl.pallas_call(
        functools.partial(kernel, n_row),
        out_shape=pltpu.VMEM((rows, cols, chan), jnp.bfloat16),
        in_specs=[hbm] * 11,
        out_specs=pl.BlockSpec(memory_space=pltpu.VMEM),
        scratch_shapes=[
            pltpu.VMEM((rows, cols, chan), jnp.bfloat16),
            pltpu.VMEM((4, 1, chan), jnp.float32),
            pltpu.VMEM((chan, 6 * hidden), jnp.bfloat16),
            pltpu.VMEM((rows, cols, hidden), jnp.bfloat16),
            pltpu.VMEM((2 * half, rows, cols, hidden), jnp.bfloat16),
            pltpu.VMEM((2, rows, cols, hidden), jnp.bfloat16),
            pltpu.VMEM((rows, cols, hidden), jnp.float32),
            pltpu.SemaphoreType.DMA((2,)),
            pltpu.SemaphoreType.DMA,
            pltpu.SemaphoreType.DMA((2,)),
            pltpu.SemaphoreType.REGULAR,
            pltpu.SemaphoreType.REGULAR,
            pltpu.VMEM((rows * cols // 2 + 4, 1, chan), jnp.float32),
            pltpu.VMEM((2 * chan, 2 * hidden), jnp.bfloat16),
        ],
        compiler_params=pltpu.CompilerParams(
            collective_id=0, has_side_effects=True, vmem_limit_bytes=16 * 2**20
        ),
    )(
        *(
            pltpu.with_memory_space_constraint(operand, pltpu.HBM)
            for operand in (
                pair_rep,
                norm_gain.reshape(1, chan),
                norm_bias.reshape(1, chan),
                w_a_proj,
                w_a_gate,
                w_b_proj,
                w_b_gate,
                w_gate,
                out_gain.reshape(1, hidden),
                out_bias.reshape(1, hidden),
                w_out,
            )
        )
    )


def body(n_row, n_sub, *operands):
    rows, cols, chan = operands[0].shape
    hidden = operands[3].shape[1]
    gathered = cols * cols * n_sub * hidden * 2
    if n_sub == 2 and n_row % 4 == 0 and cols % 16 == 0 and hidden == chan and gathered <= 4 * 2**20:
        return one_round(n_row, *operands)
    return per_device(*operands)


def solution(mesh):
    in_specs = (P(("grp", "row"), "sub", None), P(), P(), P(), P(), P(), P(), P(), P(), P(), P())
    out_specs = P(("grp", "row"), "sub", None)
    return jax.shard_map(
        functools.partial(body, mesh.shape["row"], mesh.shape["sub"]),
        mesh=mesh,
        in_specs=in_specs,
        out_specs=out_specs,
        check_vma=False,
    )
```
